256 devices in a mesh: head: 4 (over y), blk: 64 (over z, x, core).
Axes of the slice: x: 4, y: 4, z: 8, core: 2. Of those that a mesh axis runs over, the one named last changes fastest.
Arguments:
- queries: bfloat16 [64, 512, 2048], P('blk', 'head'), may hold values from -6 to 6
- keys: bfloat16 [64, 512, 256], P('blk'), may hold values from -6 to 6
- values: bfloat16 [64, 512, 256], P('blk'), may hold values from -6 to 6
- outputs: bfloat16 [64, 512, 2048], P('blk', 'head'), may hold values from -6 to 6
- output_gradient: bfloat16 [64, 512, 2048], P('blk', 'head'), may hold values from -6 to 6
- log_norms: float32 [64, 16, 512], P('blk', 'head'), may hold values from 4 to 8
- doc_lengths: int32 [32], replicated, may hold values from 1 to 4096, as said below
Outputs:
- query_grad: bfloat16 [64, 512, 2048], P('blk', 'head')
- keys_gradient: bfloat16 [64, 512, 256], P('blk', 'head')
- values_gradient: bfloat16 [64, 512, 256], P('blk', 'head')
The draws below stay inside these ranges and needn't reach their ends.
Inputs may be any that keep to these rules, and one draw needn't show every extreme that they name: `doc_lengths`: document lengths in order; they sum to 32768; the first document is the longest and holds exactly 4096 tokens.
All inputs are finite; a program needn't handle non-finite values.
Results may differ from the reference program's by a relative error of at most 0.0056.
Values may be sent and summed in bfloat16 or wider, within the bound.
A program may use at most 64 MiB of HBM per device.

```python
import jax
import jax.numpy as jnp
from jax import lax

QUERY_HEADS = 16
KEY_VALUE_HEADS = 2
HEAD_SIZE = 128
BLOCK_TOKENS = 512
SEQUENCE_BLOCKS = 64
PACKED_TOKENS = 32768
DOCUMENT_LIMIT = 4096
NDOCS = 32


def draw_doc_lengths(key, part):
    key = jax.random.fold_in(key, 7)
    other_documents = NDOCS - 1
    remaining = PACKED_TOKENS - DOCUMENT_LIMIT
    weights = jax.random.randint(key, (other_documents,), 500, 1001).astype(jnp.int32)
    total_weight = jnp.sum(weights)
    spread_tokens = remaining - other_documents
    document_portions = spread_tokens * weights // total_weight
    remainder_tokens = spread_tokens - jnp.sum(document_portions)
    extra_token_share = (jnp.arange(other_documents, dtype=jnp.int32) < remainder_tokens).astype(jnp.int32)
    residual_length = 1 + document_portions + extra_token_share
    first = jnp.full((1,), DOCUMENT_LIMIT, jnp.int32)
    return jnp.concatenate([first, residual_length.astype(jnp.int32)], axis=0)


def shard_levels(own_key, dims, cuts, low, high):
    loudness, own = 1.0, jax.random.fold_in(own_key, 6)
    for axis_at, blocks in cuts:
        steps = jnp.exp(jax.random.uniform(jax.random.fold_in(own, axis_at), (blocks,), jnp.float32, low / len(cuts), high / len(cuts)))
        loudness = loudness * jnp.repeat(steps, dims[axis_at] // blocks).reshape([-1 if axis == axis_at else 1 for axis in range(len(dims))])
    return loudness


def scatter_about(rng, shape, spread, bound, cuts=(), kind=jnp.bfloat16):
    gain = shard_levels(rng, shape, cuts, -0.22, 0.18) if cuts else 1.0
    entries = jax.random.normal(rng, shape, jnp.float32) * spread * gain
    return jnp.minimum(jnp.maximum(entries, -bound), bound).astype(kind)


def setup_inputs(seed: int = 0) -> dict:
    arg_keys = jax.random.split(jax.random.key(seed), 8)
    queries = scatter_about(arg_keys[0], (SEQUENCE_BLOCKS, BLOCK_TOKENS, QUERY_HEADS * HEAD_SIZE), 1.0, 6.0, ((0, 64), (1, 4)))
    keys = scatter_about(arg_keys[1], (SEQUENCE_BLOCKS, BLOCK_TOKENS, KEY_VALUE_HEADS * HEAD_SIZE), 1.0, 6.0, ((0, 64),))
    values = scatter_about(arg_keys[2], (SEQUENCE_BLOCKS, BLOCK_TOKENS, KEY_VALUE_HEADS * HEAD_SIZE), 1.0, 6.0, ((0, 64),))
    outputs = scatter_about(arg_keys[3], (SEQUENCE_BLOCKS, BLOCK_TOKENS, QUERY_HEADS * HEAD_SIZE), 1.0, 6.0, ((0, 64), (1, 4)))
    output_gradient = scatter_about(arg_keys[4], (SEQUENCE_BLOCKS, BLOCK_TOKENS, QUERY_HEADS * HEAD_SIZE), 1.0, 6.0, ((0, 64), (1, 4)))
    log_norms = jnp.clip(4.0 + 4.0 * jax.random.uniform(arg_keys[5], (SEQUENCE_BLOCKS, QUERY_HEADS, BLOCK_TOKENS), jnp.float32) ** shard_levels(arg_keys[5], (SEQUENCE_BLOCKS, QUERY_HEADS, BLOCK_TOKENS), ((0, 64), (1, 4)), -0.2, 0.2), 4.0, 8.0)
    doc_lengths = draw_doc_lengths(jax.random.fold_in(arg_keys[7], 71), 0)
    return {"queries": queries, "keys": keys, "values": values, "outputs": outputs, "output_gradient": output_gradient, "log_norms": log_norms, "doc_lengths": doc_lengths}


def doc_starts(doc_lengths, positions):
    firsts = jnp.cumsum(doc_lengths) - doc_lengths
    return jnp.max(jnp.where(firsts[None, :] <= positions[:, None], firsts[None, :], 0), axis=1)


def reference(queries, keys, values, outputs, output_gradient, log_norms, doc_lengths):
    query_group_size = QUERY_HEADS // KEY_VALUE_HEADS
    logit_scale = HEAD_SIZE ** -0.5
    window = DOCUMENT_LIMIT + BLOCK_TOKENS
    every_query = queries.reshape(PACKED_TOKENS, KEY_VALUE_HEADS, query_group_size, HEAD_SIZE)
    every_output = outputs.reshape(PACKED_TOKENS, KEY_VALUE_HEADS, query_group_size, HEAD_SIZE)
    output_cotangent = output_gradient.reshape(PACKED_TOKENS, KEY_VALUE_HEADS, query_group_size, HEAD_SIZE)
    leading_part = jnp.zeros((DOCUMENT_LIMIT, KEY_VALUE_HEADS, HEAD_SIZE), jnp.bfloat16)
    padded_keys = jnp.concatenate([leading_part, keys.reshape(PACKED_TOKENS, KEY_VALUE_HEADS, HEAD_SIZE)], axis=0)
    padded_values = jnp.concatenate([leading_part, values.reshape(PACKED_TOKENS, KEY_VALUE_HEADS, HEAD_SIZE)], axis=0)
    row_delta = jnp.sum(output_cotangent.astype(jnp.float32) * every_output.astype(jnp.float32), axis=-1)

    def block_step(carry, block_index):
        key_gradient_total, total_value_gradient = carry
        first_row = (block_index * BLOCK_TOKENS).astype(jnp.int32)
        query_blk = lax.dynamic_slice_in_dim(every_query, first_row, BLOCK_TOKENS, 0)
        grad_blk = lax.dynamic_slice_in_dim(output_cotangent, first_row, BLOCK_TOKENS, 0)
        delta_blk = lax.dynamic_slice_in_dim(row_delta, first_row, BLOCK_TOKENS, 0)
        key_win = lax.dynamic_slice_in_dim(padded_keys, first_row, window, 0)
        value_win = lax.dynamic_slice_in_dim(padded_values, first_row, window, 0)
        row_statistics = lax.dynamic_index_in_dim(log_norms, block_index, 0, keepdims=False)
        row_statistics = row_statistics.reshape(KEY_VALUE_HEADS, query_group_size, BLOCK_TOKENS)
        query_pos = first_row + jnp.arange(BLOCK_TOKENS, dtype=jnp.int32)
        key_pos = first_row - DOCUMENT_LIMIT + jnp.arange(window, dtype=jnp.int32)
        first_pos = doc_starts(doc_lengths, query_pos)
        allowed = (key_pos[None, :] <= query_pos[:, None]) & (key_pos[None, :] >= first_pos[:, None])
        scores = logit_scale * jnp.einsum('qkgd,wkd->kgqw', query_blk.astype(jnp.float32), key_win.astype(jnp.float32))
        probability = jnp.where(allowed[None, None], jnp.exp(scores - row_statistics[..., None]), 0.0)
        prob_low = probability.astype(jnp.bfloat16)
        value_add = jnp.einsum('kgqw,qkgd->wkd', prob_low.astype(jnp.float32), grad_blk.astype(jnp.float32))
        dprob = jnp.einsum('qkgd,wkd->kgqw', grad_blk.astype(jnp.float32), value_win.astype(jnp.float32))
        dscore = (probability * (dprob - jnp.transpose(delta_blk, (1, 2, 0))[..., None])).astype(jnp.bfloat16)
        query_out = (logit_scale * jnp.einsum('kgqw,wkd->qkgd', dscore.astype(jnp.float32), key_win.astype(jnp.float32))).astype(jnp.bfloat16)
        key_increment = jnp.einsum('kgqw,qkgd->wkd', dscore.astype(jnp.float32), query_blk.astype(jnp.float32))
        key_gradient_total = lax.dynamic_update_slice_in_dim(key_gradient_total, lax.dynamic_slice_in_dim(key_gradient_total, first_row, window, 0) + key_increment, first_row, 0)
        total_value_gradient = lax.dynamic_update_slice_in_dim(total_value_gradient, lax.dynamic_slice_in_dim(total_value_gradient, first_row, window, 0) + value_add, first_row, 0)
        return (key_gradient_total, total_value_gradient), query_out

    blank_tensor = jnp.zeros((DOCUMENT_LIMIT + PACKED_TOKENS, KEY_VALUE_HEADS, HEAD_SIZE), jnp.float32)
    (key_gradient_total, total_value_gradient), query_blocks = lax.scan(block_step, (blank_tensor, blank_tensor), jnp.arange(SEQUENCE_BLOCKS, dtype=jnp.int32))
    query_grad = query_blocks.reshape(SEQUENCE_BLOCKS, BLOCK_TOKENS, QUERY_HEADS * HEAD_SIZE)
    keys_gradient = (logit_scale * key_gradient_total[DOCUMENT_LIMIT:]).astype(jnp.bfloat16).reshape(SEQUENCE_BLOCKS, BLOCK_TOKENS, KEY_VALUE_HEADS * HEAD_SIZE)
    values_gradient = total_value_gradient[DOCUMENT_LIMIT:].astype(jnp.bfloat16).reshape(SEQUENCE_BLOCKS, BLOCK_TOKENS, KEY_VALUE_HEADS * HEAD_SIZE)
    return query_grad, keys_gradient, values_gradient
```

```python
import functools

import jax
import jax.numpy as jnp
from jax import lax
from jax.experimental import pallas as pl
from jax.experimental.pallas import tpu as pltpu
from jax.sharding import PartitionSpec as P

QUERY_HEADS = 16
KEY_VALUE_HEADS = 2
BF = jnp.bfloat16
F32 = jnp.float32
SCALE = 128**-0.5
EXP2_SCALE = SCALE * 1.4426950408889634
FAR = 16384.0
MESH = pl.DeviceIdType.MESH


def split3(x):
    hi = x.astype(BF).astype(F32)
    rest = x - hi
    mid = rest.astype(BF).astype(F32)
    return hi, mid, rest - mid


def kernel(
    q_ref, k_ref, v_ref, o_ref, g_ref, lse_ref, len_ref,
    dq_ref, dk_ref, dv_ref,
    kvs, pst, sin, inbox, tot, ysend, yin, lse_all,
    qn, gn, qta, gta, dqt, kt, dk, dv,
    s_next, s_far, s_two, s_sib, r_kv,
    s_psib, r_psib, s_pout, r_pout,
    s_lse, r_lse, s_y, r_y,
):
    y = lax.axis_index("head")
    b = lax.axis_index("blk")
    r = lax.rem(b, 2)
    c = b // 2
    row0 = b < 8
    cs = jnp.where(row0, c, c - 4)
    last = jnp.where(row0, 3, 27)
    core0, core1 = r == 0, r == 1
    prev1, next1 = cs >= 1, cs <= last - 1
    row0_prev2 = row0 & (cs >= 2)
    row0_next2 = row0 & (cs <= 1)
    rows_prev2 = jnp.logical_not(row0) & (cs >= 2) & core0
    rows_next2 = jnp.logical_not(row0) & (cs <= last - 2) & core1
    first_chip = row0 & (cs == 0)
    last_chip = row0 & (cs == 3)
    sib = b + 1 - 2 * r
    middle = row0 & (cs >= 1) & (cs <= 2)

    def copy(src, dst, send, recv, blk):
        return pltpu.make_async_remote_copy(
            src_ref=src, dst_ref=dst, send_sem=send, recv_sem=recv,
            device_id={"blk": blk}, device_id_type=MESH,
        )

    def kv_copy(src, dst, j, send, blk):
        return copy(kvs.at[src, j], kvs.at[dst, j], send.at[j], r_kv.at[dst, j], blk)

    def kv_wait(slot, j):
        copy(kvs.at[slot, j], kvs.at[slot, j], s_next.at[j], r_kv.at[slot, j], sib).wait_recv()

    def sib_slot(e):
        return jnp.where(core0, e + 1, e - 1)

    def odd_slot(e):
        return jnp.where(core0, e - 1, e + 1)

    def sib_copy(e, j):
        return copy(
            kvs.at[e, j], kvs.at[sib_slot(e), j], s_sib.at[e // 2, j], r_kv.at[sib_slot(e), j], sib
        )

    for j in range(2):
        kvs[0, j, 0] = k_ref[0, :, j * 128 : (j + 1) * 128]
        kvs[0, j, 1] = v_ref[0, :, j * 128 : (j + 1) * 128]

    barrier = pltpu.get_barrier_semaphore()

    def greet(cond, blk):
        @pl.when(cond)
        def _():
            pl.semaphore_signal(barrier, inc=1, device_id={"blk": blk}, device_id_type=MESH)

        return jnp.where(cond, 1, 0)

    partners = greet(b >= 0, sib)
    partners += greet(prev1, b - 2)
    partners += greet(next1, b + 2)
    partners += greet(row0_prev2, b - 4)
    partners += greet(row0_next2, b + 4)
    partners += greet(rows_prev2, b - 3)
    partners += greet(rows_next2, b + 3)
    partners += greet(first_chip, b + 6)
    partners += greet(last_chip, b - 6)
    for i in range(1, 4):
        pl.semaphore_signal(
            barrier, inc=1, device_id={"head": lax.rem(y + i, 4)}, device_id_type=MESH
        )
    pl.semaphore_wait(barrier, partners + 3)

    def lse_copy(i):
        peer = lax.rem(y + i, 4)
        return pltpu.make_async_remote_copy(
            src_ref=lse_ref.at[0, :, pl.ds(pl.multiple_of(peer * 128, 128), 128)],
            dst_ref=lse_all.at[i],
            send_sem=s_lse.at[i], recv_sem=r_lse.at[i],
            device_id={"head": peer}, device_id_type=MESH,
        )

    for i in range(1, 4):
        lse_copy(i).start()

    def own_sends(act):
        for j in range(2):
            @pl.when(core0)
            def _():
                act(sib_copy(0, j))

            @pl.when(next1)
            def _():
                act(kv_copy(0, 2, j, s_next, b + 2))

            @pl.when(first_chip)
            def _():
                act(kv_copy(0, 6, j, s_far, b + 6))

        for j in range(2):
            @pl.when(rows_next2)
            def _():
                act(kv_copy(0, 3, j, s_two, b + 3))

    own_sends(lambda d: d.start())

    lane = lax.broadcasted_iota(jnp.int32, (8, 128), 1)
    row = lax.broadcasted_iota(jnp.int32, (32, 128), 0)
    lo_l = jnp.zeros((8, 128), jnp.int32)
    len_l = jnp.zeros((8, 128), jnp.int32)
    lo_r = jnp.zeros((32, 128), jnp.int32)
    len_r = jnp.zeros((32, 128), jnp.int32)
    for i in range(32):
        n = len_ref[i]
        lo_l += jnp.where(lane > i, n, 0)
        len_l += jnp.where(lane == i, n, 0)
        lo_r += jnp.where(row > i, n, 0)
        len_r += jnp.where(row == i, n, 0)
    hi_l = lo_l + len_l
    qpos = b * 512 + y * 128 + lax.broadcasted_iota(jnp.int32, (32, 128), 1)
    doc_rows = jnp.where((qpos >= lo_r) & (qpos < lo_r + len_r), 0.0, -FAR)
    doc_rows = jnp.concatenate([doc_rows, jnp.zeros((96, 128), F32)], 0)
    aug_row = lax.broadcasted_iota(jnp.int32, (128, 128), 0)

    for h in range(QUERY_HEADS):
        ch, o = h // 2, (h % 2) * 128
        qh = q_ref[0, :, h * 128 : (h + 1) * 128]
        gh = g_ref[0, :, h * 128 : (h + 1) * 128]
        oh = o_ref[0, :, h * 128 : (h + 1) * 128]
        gt = gh.T
        qn[ch, o : o + 128, :] = qh
        gn[ch, o : o + 128, :] = gh
        qta[ch, 0:128, o : o + 128] = qh.T
        gta[ch, 0:128, o : o + 128] = gt
        delta = jnp.sum(gt.astype(F32) * oh.T.astype(F32), axis=0, keepdims=True)
        d0, d1, d2 = split3(-delta)
        aug = jnp.where(aug_row == 32, d0, 0.0)
        aug = jnp.where(aug_row == 33, d1, aug)
        aug = jnp.where(aug_row == 34, d2, aug)
        gta[ch, 128:256, o : o + 128] = aug.astype(BF)
    dqt[...] = jnp.zeros_like(dqt)

    lse_all[0] = lse_ref[0, :, pl.ds(pl.multiple_of(y * 128, 128), 128)]
    for i in range(1, 4):
        lse_copy(i).wait()
    for h in range(QUERY_HEADS):
        ch, o = h // 2, (h % 2) * 128
        came = lax.rem(y + 4 - h // 4, 4)
        stat = lse_all[came, h % 4 : h % 4 + 1, :] * (-(128.0**0.5))
        d0, d1, d2 = split3(stat)
        aug = jnp.where(aug_row == 32, d0, doc_rows)
        aug = jnp.where(aug_row == 33, d1, aug)
        aug = jnp.where(aug_row == 34, d2, aug)
        qta[ch, 128:256, o : o + 128] = aug.astype(BF)

    def tile(d, j, causal):
        lane_k = lax.broadcasted_iota(jnp.int32, (512, 128), 1)
        kpos = (b - d) * 512 + lax.broadcasted_iota(jnp.int32, (512, 128), 0)
        inside = (kpos >= lo_l[0:1]) & (kpos < hi_l[0:1])
        ones = (lane_k >= 32) & (lane_k < 35)
        aug = jnp.where(inside | ones, 1.0, 0.0).astype(BF)
        k = kvs[d, j, 0]
        kj = jnp.concatenate([k, aug], 1)
        vj = jnp.concatenate([kvs[d, j, 1], aug], 1)
        kt[...] = k.T
        for i in range(4):
            ch = j * 4 + i
            st = jnp.dot(kj, qta[ch], preferred_element_type=F32)
            p = jnp.exp2(st * EXP2_SCALE)
            if causal:
                krow = lax.broadcasted_iota(jnp.int32, (512, 256), 0)
                qcol = lax.broadcasted_iota(jnp.int32, (512, 256), 1) & 127
                p = jnp.where(krow <= qcol + y * 128, p, 0.0)
            dp = jnp.dot(vj, gta[ch], preferred_element_type=F32)
            ds = (p * dp).astype(BF)
            dvi = jnp.dot(p.astype(BF), gn[ch], preferred_element_type=F32)
            dki = jnp.dot(ds, qn[ch], preferred_element_type=F32)
            if i == 0:
                dv[...] = dvi
                dk[...] = dki
            else:
                dv[...] += dvi
                dk[...] += dki
            dqt[ch] += jnp.dot(kt[...], ds, preferred_element_type=F32)
        if causal:
            tot[j, 0] = dk[...]
            tot[j, 1] = dv[...]
        else:
            pst[d, j, 0] = dk[...].astype(BF)
            pst[d, j, 1] = dv[...].astype(BF)

    def psib_copy(d, j):
        e = jnp.where(core0, d + 1, d - 1)
        return copy(pst.at[d, j], sin.at[e // 2, j], s_psib.at[d // 2, j], r_psib.at[e // 2, j], sib)

    def psib_wait(e, j):
        copy(
            sin.at[e // 2, j], sin.at[e // 2, j], s_psib.at[0, j], r_psib.at[e // 2, j], sib
        ).wait_recv()

    def out_copy(e, j, kind, blk):
        return copy(pst.at[e, j], inbox.at[kind, j], s_pout.at[kind, j], r_pout.at[kind, j], blk)

    def in_wait(kind, j):
        copy(
            inbox.at[kind, j], inbox.at[kind, j], s_pout.at[kind, j], r_pout.at[kind, j], sib
        ).wait_recv()

    def merge_out(e, j, kind, blk):
        psib_wait(e, j)
        pst[e, j] = (pst[e, j].astype(F32) + sin[e // 2, j].astype(F32)).astype(BF)
        out_copy(e, j, kind, blk).start()

    def own_block(j, carry):
        tile(0, j, True)

        return carry

    lax.fori_loop(0, 2, own_block, 0)

    def run(d, j):
        tile(d, j, False)

    def sibling_block(j, carry):
        kv_wait(1, j)
        run(1, j)
        psib_copy(1, j).start()
        return carry

    @pl.when(core1)
    def _():
        lax.fori_loop(0, 2, sibling_block, 0)

    far_count = jnp.where(last_chip, 2, 1)

    def near(j, carry):
        kv_wait(2, j)

        @pl.when(middle & next1)
        def _():
            kv_copy(2, 4, j, s_two, b + 2).start()

        sib_copy(2, j).start()

        @pl.when(last_chip)
        def _():
            kv_wait(6, j)
            sib_copy(6, j).start()

        def even(i, carry):
            run(2 + 4 * i, j)
            return carry

        lax.fori_loop(0, far_count, even, 0)

        def odd(i, carry):
            d = odd_slot(2 + 4 * i)
            kv_wait(d, j)
            run(d, j)
            psib_copy(d, j).start()
            return carry

        lax.fori_loop(0, far_count, odd, 0)
        merge_out(2, j, 0, b - 2)

        @pl.when(last_chip)
        def _():
            merge_out(6, j, 2, b - 6)

        return carry

    @pl.when(prev1)
    def _():
        lax.fori_loop(0, 2, near, 0)

    def two_row0(j, carry):
        kv_wait(4, j)
        sib_copy(4, j).start()
        run(4, j)
        d = odd_slot(4)
        kv_wait(d, j)
        run(d, j)
        psib_copy(d, j).start()
        merge_out(4, j, 1, b - 4)
        return carry

    @pl.when(row0_prev2)
    def _():
        lax.fori_loop(0, 2, two_row0, 0)

    def two_rows(j, carry):
        kv_wait(3, j)
        run(3, j)
        out_copy(3, j, 1, b - 3).start()
        return carry

    @pl.when(rows_prev2)
    def _():
        lax.fori_loop(0, 2, two_rows, 0)

    for h in range(QUERY_HEADS):
        ch, o = h // 2, (h % 2) * 128
        dq_ref[0, :, h * 128 : (h + 1) * 128] = (dqt[ch, :, o : o + 128] * SCALE).T.astype(BF)

    def y_copy(i, j):
        peer = lax.rem(y + i, 4)
        return pltpu.make_async_remote_copy(
            src_ref=ysend.at[j, peer], dst_ref=yin.at[j, i],
            send_sem=s_y.at[j, i], recv_sem=r_y.at[j, i],
            device_id={"head": peer}, device_id_type=MESH,
        )

    def add_up(j, carry):
        @pl.when(core0)
        def _():
            psib_wait(0, j)
            tot[j] += sin[0, j].astype(F32)

        @pl.when(next1)
        def _():
            in_wait(0, j)
            tot[j] += inbox[0, j].astype(F32)

        @pl.when(row0_next2 | rows_next2)
        def _():
            in_wait(1, j)
            tot[j] += inbox[1, j].astype(F32)

        @pl.when(first_chip)
        def _():
            in_wait(2, j)
            tot[j] += inbox[2, j].astype(F32)

        for part in range(4):
            ysend[j, part] = tot[j, :, part * 128 : (part + 1) * 128, :].astype(BF)
        for i in range(1, 4):
            y_copy(i, j).start()
        return carry

    lax.fori_loop(0, 2, add_up, 0)
    mine = pl.ds(pl.multiple_of(y * 128, 128), 128)
    for j in range(2):
        total = tot[j, :, mine, :]
        for i in range(1, 4):
            y_copy(i, j).wait()
            total = total + yin[j, i].astype(F32)
        dk_ref[0, :, j * 128 : (j + 1) * 128] = (total[0] * SCALE).astype(BF)
        dv_ref[0, :, j * 128 : (j + 1) * 128] = total[1].astype(BF)

    own_sends(lambda d: d.wait_send())
    for j in range(2):
        @pl.when(core1)
        def _():
            psib_copy(1, j).wait_send()

        @pl.when(prev1)
        def _():
            sib_copy(2, j).wait_send()
            psib_copy(odd_slot(2), j).wait_send()
            out_copy(2, j, 0, b - 2).wait_send()

        @pl.when(middle & next1)
        def _():
            kv_copy(2, 4, j, s_two, b + 2).wait_send()

        @pl.when(last_chip)
        def _():
            sib_copy(6, j).wait_send()
            psib_copy(odd_slot(6), j).wait_send()
            out_copy(6, j, 2, b - 6).wait_send()

        @pl.when(row0_prev2)
        def _():
            sib_copy(4, j).wait_send()
            psib_copy(odd_slot(4), j).wait_send()
            out_copy(4, j, 1, b - 4).wait_send()

        @pl.when(rows_prev2)
        def _():
            out_copy(3, j, 1, b - 3).wait_send()


def fused(queries, keys, values, outputs, output_gradient, log_norms, doc_lengths):
    vmem = pl.BlockSpec(memory_space=pltpu.VMEM)
    dma = pltpu.SemaphoreType.DMA
    return pl.pallas_call(
        kernel,
        out_shape=(
            jax.ShapeDtypeStruct((1, 128, 2048), BF),
            jax.ShapeDtypeStruct((1, 128, 256), BF),
            jax.ShapeDtypeStruct((1, 128, 256), BF),
        ),
        in_specs=[vmem] * 6 + [pl.BlockSpec(memory_space=pltpu.SMEM)],
        out_specs=(vmem, vmem, vmem),
        scratch_shapes=[
            pltpu.VMEM((8, 2, 2, 512, 128), BF),
            pltpu.VMEM((8, 2, 2, 512, 128), BF),
            pltpu.VMEM((4, 2, 2, 512, 128), BF),
            pltpu.VMEM((3, 2, 2, 512, 128), BF),
            pltpu.VMEM((2, 2, 512, 128), F32),
            pltpu.VMEM((2, 4, 2, 128, 128), BF),
            pltpu.VMEM((2, 4, 2, 128, 128), BF),
            pltpu.VMEM((4, 4, 128), F32),
            pltpu.VMEM((8, 256, 128), BF),
            pltpu.VMEM((8, 256, 128), BF),
            pltpu.VMEM((8, 256, 256), BF),
            pltpu.VMEM((8, 256, 256), BF),
            pltpu.VMEM((8, 128, 256), F32),
            pltpu.VMEM((128, 512), BF),
            pltpu.VMEM((512, 128), F32),
            pltpu.VMEM((512, 128), F32),
            dma((2,)), dma((2,)), dma((2,)), dma((4, 2)), dma((8, 2)),
            dma((4, 2)), dma((4, 2)), dma((3, 2)), dma((3, 2)),
            dma((4,)), dma((4,)), dma((2, 4)), dma((2, 4)),
        ],
        compiler_params=pltpu.CompilerParams(
            collective_id=0, has_side_effects=True, vmem_limit_bytes=56 * 2**20
        ),
    )(queries, keys, values, outputs, output_gradient, log_norms, doc_lengths)


def passed_along(x, axis, by):
    peers = lax.axis_size(axis)
    return lax.ppermute(x, axis, [(i, (i + by) % peers) for i in range(peers)])


def shifted(block, axis, distance):
    devices = range(lax.axis_size(axis))
    route = [(i - distance, i) for i in devices if i - distance in devices]
    return lax.ppermute(block, axis, route)


def doc_starts(doc_lengths, positions):
    firsts = jnp.cumsum(doc_lengths) - doc_lengths
    return jnp.max(jnp.where(firsts[None, :] <= positions[:, None], firsts[None, :], 0), axis=1)


def pass_grads(key_gradient_total, total_value_gradient):
    return passed_along((key_gradient_total, total_value_gradient), "blk", 1)


def ring(queries, keys, values, outputs, output_gradient, log_norms, doc_lengths):
    block_count = lax.axis_size("blk")
    block_index = lax.axis_index("blk")
    every_query, every_output, grad_all = (
        lax.all_to_all(queries, "head", split_axis=2, concat_axis=1, tiled=True),
        lax.all_to_all(outputs, "head", split_axis=2, concat_axis=1, tiled=True),
        lax.all_to_all(output_gradient, "head", split_axis=2, concat_axis=1, tiled=True),
    )
    rows_per_block = every_query.shape[1]
    head_features = keys.shape[2] // KEY_VALUE_HEADS
    local_heads = every_query.shape[2] // head_features
    query_group_size = QUERY_HEADS // KEY_VALUE_HEADS
    logit_scale = head_features ** (-0.5)
    query_loc = every_query[0].reshape(rows_per_block, local_heads, head_features)
    grad_loc = grad_all[0].reshape(rows_per_block, local_heads, head_features)
    output_loc = every_output[0].reshape(rows_per_block, local_heads, head_features)
    row_delta = jnp.sum(grad_loc.astype(jnp.float32) * output_loc.astype(jnp.float32), axis=-1).T
    row_statistics = log_norms[0]
    kv_head = lax.axis_index("head") * local_heads // query_group_size
    key_own = lax.dynamic_slice_in_dim(keys[0], kv_head * head_features, head_features, 1)
    value_own = lax.dynamic_slice_in_dim(values[0], kv_head * head_features, head_features, 1)
    query_pos = block_index * rows_per_block + jnp.arange(rows_per_block, dtype=jnp.int32)
    first_pos = doc_starts(doc_lengths, query_pos)

    def tile_grads(pair, key_block):
        key_blk, value_blk = pair
        key_pos = key_block * rows_per_block + jnp.arange(rows_per_block, dtype=jnp.int32)
        allowed = (key_pos[None, :] <= query_pos[:, None]) & (
            key_pos[None, :] >= first_pos[:, None]
        )
        scores = logit_scale * jnp.einsum(
            "qhd,kd->hqk", query_loc, key_blk, preferred_element_type=jnp.float32
        )
        probability = jnp.where(allowed[None], jnp.exp(scores - row_statistics[:, :, None]), 0.0)
        prob_low = probability.astype(jnp.bfloat16)
        value_add = jnp.einsum(
            "hqk,qhd->kd", prob_low, grad_loc, preferred_element_type=jnp.float32
        )
        dprob = jnp.einsum("qhd,kd->hqk", grad_loc, value_blk, preferred_element_type=jnp.float32)
        dscore = (probability * (dprob - row_delta[:, :, None])).astype(jnp.bfloat16)
        query_add = jnp.einsum("hqk,kd->qhd", dscore, key_blk, preferred_element_type=jnp.float32)
        key_increment = jnp.einsum(
            "hqk,qhd->kd", dscore, query_loc, preferred_element_type=jnp.float32
        )
        return (query_add, key_increment, value_add)

    def no_grads():
        flat = jnp.zeros((rows_per_block, head_features), jnp.float32)
        return (jnp.zeros((rows_per_block, local_heads, head_features), jnp.float32), flat, flat)

    def visit_block(carry_state, cycle_step):
        pair, query_acc, key_gradient_total, total_value_gradient = carry_state
        key_block = (block_index - cycle_step) % block_count
        active = (key_block <= block_index) & ((key_block + 1) * rows_per_block - 1 >= first_pos[0])
        query_add, key_increment, value_add = lax.cond(
            active, lambda: tile_grads(pair, key_block), no_grads
        )
        return (
            pair,
            query_acc + query_add,
            key_gradient_total + key_increment,
            total_value_gradient + value_add,
        )

    def cycle_turn(cycle_step, carry_state):
        pair, query_acc, key_gradient_total, total_value_gradient = visit_block(
            carry_state, cycle_step
        )
        pair = shifted((pair[0], pair[1]), "blk", 1)
        key_gradient_total, total_value_gradient = pass_grads(
            key_gradient_total, total_value_gradient
        )
        return (pair, query_acc, key_gradient_total, total_value_gradient)

    flat_zero = jnp.zeros((rows_per_block, head_features), jnp.float32)
    initial = (
        (key_own, value_own),
        jnp.zeros((rows_per_block, local_heads, head_features), jnp.float32),
        flat_zero,
        flat_zero,
    )
    carry_state = lax.fori_loop(0, block_count - 1, cycle_turn, initial)
    pair, query_acc, key_gradient_total, total_value_gradient = visit_block(
        carry_state, block_count - 1
    )
    key_gradient_total, total_value_gradient = pass_grads(key_gradient_total, total_value_gradient)
    broad_zeros = jnp.zeros((rows_per_block, KEY_VALUE_HEADS * head_features), jnp.float32)
    key_broadcast = lax.dynamic_update_slice_in_dim(
        broad_zeros, key_gradient_total, kv_head * head_features, 1
    )
    value_wide = lax.dynamic_update_slice_in_dim(
        broad_zeros, total_value_gradient, kv_head * head_features, 1
    )
    key_part, value_part = (
        lax.psum_scatter(key_broadcast, "head", scatter_dimension=0, tiled=True),
        lax.psum_scatter(value_wide, "head", scatter_dimension=0, tiled=True),
    )
    keys_gradient = (logit_scale * key_part).astype(jnp.bfloat16)[None]
    values_gradient = value_part.astype(jnp.bfloat16)[None]
    query_out = (
        (logit_scale * query_acc)
        .astype(jnp.bfloat16)
        .reshape(1, rows_per_block, local_heads * head_features)
    )
    query_grad = lax.all_to_all(query_out, "head", split_axis=1, concat_axis=2, tiled=True)
    return (query_grad, keys_gradient, values_gradient)


def shards(*arrays):
    short = jnp.max(arrays[-1][1:]) <= 1537
    return lax.cond(short, fused, ring, *arrays)


def solution(mesh):
    in_specs = (
        P("blk", "head", None),
        P("blk", None, None),
        P("blk", None, None),
        P("blk", "head", None),
        P("blk", "head", None),
        P("blk", "head", None),
        P(),
    )
    out_specs = (P("blk", "head", None), P("blk", "head", None), P("blk", "head", None))
    return jax.shard_map(shards, mesh=mesh, in_specs=in_specs, out_specs=out_specs, check_vma=False)
```

```python
import functools

import jax
import jax.numpy as jnp
from jax import lax
from jax.experimental import pallas as pl
from jax.experimental.pallas import tpu as pltpu
from jax.sharding import PartitionSpec as P

QUERY_HEADS = 16
KEY_VALUE_HEADS = 2
BF = jnp.bfloat16
F32 = jnp.float32
SCALE = 128**-0.5
EXP2_SCALE = SCALE * 1.4426950408889634
FAR = 16384.0
MESH = pl.DeviceIdType.MESH


def split3(x):
    hi = x.astype(BF).astype(F32)
    rest = x - hi
    mid = rest.astype(BF).astype(F32)
    return hi, mid, rest - mid


def kernel(
    q_ref, k_ref, v_ref, o_ref, g_ref, lse_ref, len_ref,
    dq_ref, dk_ref, dv_ref,
    kvs, other, first_out, first_in, second_out, second_in, kept, last_out, last_in, mine,
    lse_all, swap, dq_out, dq_in,
    qn, gn, qta, gta, dqt, kt, dk, dv, aug,
    s_own, s_next, s_far, s_two, s_pass, r_kv,
    s_first, r_first, s_second, r_second, s_last, r_last,
    s_lse, r_lse, s_swap, r_swap, s_dq, r_dq,
):
    y = lax.axis_index("head")
    b = lax.axis_index("blk")
    r = lax.rem(b, 2)
    sr = 1 - r
    c = b // 2
    row0 = b < 8
    rows = b >= 8
    cs = jnp.where(row0, c, c - 4)
    last = jnp.where(row0, 3, 27)
    prev1, next1 = cs >= 1, cs <= last - 1
    prev2, next2 = cs >= 2, cs <= last - 2
    first_chip = row0 & (cs == 0)
    last_chip = row0 & (cs == 3)
    passes = row0 & prev1 & next1
    sib = 2 * c + sr

    def copy(src, dst, send, recv, blk):
        return pltpu.make_async_remote_copy(
            src_ref=src, dst_ref=dst, send_sem=send, recv_sem=recv,
            device_id={"blk": blk}, device_id_type=MESH,
        )

    def pack(ref, head):
        cols = pl.ds(pl.multiple_of(head * 128, 128), 128)
        ref[0] = k_ref[0, :, cols]
        ref[1] = v_ref[0, :, cols]

    pack(kvs.at[r], r)
    pack(other, sr)

    barrier = pltpu.get_barrier_semaphore()

    def greet(cond, blk):
        @pl.when(cond)
        def _():
            for core in range(2):
                pl.semaphore_signal(
                    barrier, inc=1, device_id={"blk": blk + core}, device_id_type=MESH
                )

        return jnp.where(cond, 2, 0)

    pl.semaphore_signal(barrier, inc=1, device_id={"blk": sib}, device_id_type=MESH)
    partners = 1 + greet(prev1, 2 * c - 2)
    partners += greet(next1, 2 * c + 2)
    partners += greet(prev2, 2 * c - 4)
    partners += greet(next2, 2 * c + 4)
    partners += greet(first_chip, 2 * c + 6)
    partners += greet(last_chip, 2 * c - 6)
    for i in range(1, 4):
        for core in range(2):
            pl.semaphore_signal(
                barrier, inc=1, device_id=(lax.rem(y + i, 4), 2 * c + core), device_id_type=MESH
            )
    pl.semaphore_wait(barrier, partners + 6)

    def to_chip(dist, slot, sems):
        return (
            copy(kvs.at[r], kvs.at[slot], sems.at[0], r_kv.at[slot], 2 * (c + dist) + r),
            copy(other, kvs.at[slot], sems.at[1], r_kv.at[slot], 2 * (c + dist) + sr),
        )

    own_copy = copy(other, kvs.at[r], s_own, r_kv.at[r], sib)

    def kv_wait(slot):
        copy(kvs.at[slot], kvs.at[slot], s_own, r_kv.at[slot], sib).wait_recv()

    def pass_copy(slot):
        p = lax.rem(slot, 2)
        return copy(kvs.at[slot], kvs.at[slot + 2], s_pass.at[p], r_kv.at[slot + 2], b + 2)

    def swap_copy(i):
        src = (q_ref, g_ref, o_ref)[i]
        cols = pl.ds(pl.multiple_of(sr * 1024, 1024), 1024)
        return copy(src.at[0, :, cols], swap.at[i], s_swap.at[i], r_swap.at[i], sib)

    stat_core = y // 2
    stat_here = r == stat_core

    def lse_tokens(peer):
        return lse_ref.at[0, :, pl.ds(pl.multiple_of(peer * 128, 128), 128)]

    def lse_copy(i):
        peer = lax.rem(y + i, 4)
        return pltpu.make_async_remote_copy(
            src_ref=lse_tokens(peer), dst_ref=lse_all.at[r, lax.rem(y, 2)],
            send_sem=s_lse.at[i], recv_sem=r_lse.at[r, lax.rem(y, 2)],
            device_id=(peer, 2 * c + stat_core), device_id_type=MESH,
        )

    @pl.when(next1)
    def _():
        for d in to_chip(1, 2 + r, s_next):
            d.start()

    @pl.when(first_chip)
    def _():
        for d in to_chip(3, 6 + r, s_far):
            d.start()

    for i in range(1, 4):
        lse_copy(i).start()

    @pl.when(stat_here)
    def _():
        lse_all[r, lax.rem(y, 2)] = lse_tokens(y)[...]

    @pl.when(jnp.logical_not(stat_here))
    def _():
        lse_copy(0).start()

    for i in range(3):
        swap_copy(i).start()
    own_copy.start()

    lane = lax.broadcasted_iota(jnp.int32, (8, 128), 1)
    row = lax.broadcasted_iota(jnp.int32, (32, 128), 0)
    lo_l = jnp.zeros((8, 128), jnp.int32)
    len_l = jnp.zeros((8, 128), jnp.int32)
    lo_r = jnp.zeros((32, 128), jnp.int32)
    len_r = jnp.zeros((32, 128), jnp.int32)
    for i in range(32):
        n = len_ref[i]
        lo_l += jnp.where(lane > i, n, 0)
        len_l += jnp.where(lane == i, n, 0)
        lo_r += jnp.where(row > i, n, 0)
        len_r += jnp.where(row == i, n, 0)
    hi_l = lo_l + len_l
    aug_row = lax.broadcasted_iota(jnp.int32, (128, 128), 0)

    def prepare(block, q_of, g_of, o_of):
        qpos = (2 * c + block) * 512 + y * 128 + lax.broadcasted_iota(jnp.int32, (32, 128), 1)
        doc_rows = jnp.where((qpos >= lo_r) & (qpos < lo_r + len_r), 0.0, -FAR)
        doc_rows = jnp.concatenate([doc_rows, jnp.zeros((96, 128), F32)], 0)
        for h in range(8):
            ch, o = block * 4 + h // 2, (h % 2) * 128
            qh, gh, oh = q_of(h), g_of(h), o_of(h)
            gt = gh.T
            qn[ch, o : o + 128, :] = qh
            gn[ch, o : o + 128, :] = gh
            qta[ch, 0:128, o : o + 128] = qh.T
            gta[ch, 0:128, o : o + 128] = gt
            delta = jnp.sum(gt.astype(F32) * oh.T.astype(F32), axis=0, keepdims=True)
            d0, d1, d2 = split3(-delta)
            extra = jnp.where(aug_row == 32, d0, 0.0)
            extra = jnp.where(aug_row == 33, d1, extra)
            extra = jnp.where(aug_row == 34, d2, extra)
            gta[ch, 128:256, o : o + 128] = extra.astype(BF)
            stat = lse_all[block, h // 4, h % 4 : h % 4 + 1, :] * (-(128.0**0.5))
            d0, d1, d2 = split3(stat)
            extra = jnp.where(aug_row == 32, d0, doc_rows)
            extra = jnp.where(aug_row == 33, d1, extra)
            extra = jnp.where(aug_row == 34, d2, extra)
            qta[ch, 128:256, o : o + 128] = extra.astype(BF)

    def own_head(ref):
        return lambda h: ref[0, :, pl.ds(pl.multiple_of(r * 1024 + h * 128, 128), 128)]

    def swapped(i):
        return lambda h: swap[i, :, h * 128 : (h + 1) * 128]

    def lse_wait(block, half):
        @pl.when(jnp.logical_not((block == r) & (y == 2 * r + half)))
        def _():
            pltpu.make_async_remote_copy(
                src_ref=lse_all.at[block, half], dst_ref=lse_all.at[block, half],
                send_sem=s_lse.at[0], recv_sem=r_lse.at[block, half],
                device_id=(y, sib), device_id_type=MESH,
            ).wait_recv()

    dqt[...] = jnp.zeros_like(dqt)
    for block in range(2):
        for half in range(2):
            lse_wait(block, half)
    prepare(r, own_head(q_ref), own_head(g_ref), own_head(o_ref))
    for i in range(3):
        swap_copy(i).wait_recv()
    prepare(sr, swapped(0), swapped(1), swapped(2))

    def tile(slot):
        lane_k = lax.broadcasted_iota(jnp.int32, (512, 128), 1)
        kpos = (2 * (c - slot // 2) + lax.rem(slot, 2)) * 512
        kpos = kpos + lax.broadcasted_iota(jnp.int32, (512, 128), 0)
        inside = (kpos >= lo_l[0:1]) & (kpos < hi_l[0:1])
        ones = (lane_k >= 32) & (lane_k < 35)
        aug[...] = jnp.where(inside | ones, 1.0, 0.0).astype(BF)
        kt[...] = kvs[slot, 0].T
        dk[...] = jnp.zeros_like(dk)
        dv[...] = jnp.zeros_like(dv)

        def part(block, causal):
            kj = jnp.concatenate([kvs[slot, 0], aug[...]], 1)
            vj = jnp.concatenate([kvs[slot, 1], aug[...]], 1)
            for i in range(4):
                ch = block * 4 + i
                st = jnp.dot(kj, qta[ch], preferred_element_type=F32)
                p = jnp.exp2(st * EXP2_SCALE)
                if causal:
                    krow = lax.broadcasted_iota(jnp.int32, (512, 256), 0)
                    qcol = lax.broadcasted_iota(jnp.int32, (512, 256), 1) & 127
                    p = jnp.where(krow <= qcol + y * 128, p, 0.0)
                dp = jnp.dot(vj, gta[ch], preferred_element_type=F32)
                ds = (p * dp).astype(BF)
                dv[...] += jnp.dot(p.astype(BF), gn[ch], preferred_element_type=F32)
                dk[...] += jnp.dot(ds, qn[ch], preferred_element_type=F32)
                dqt[ch] += jnp.dot(kt[...], ds, preferred_element_type=F32)

        @pl.when(slot < 2)
        def _():
            part(slot, True)

        low = jnp.where(slot < 2, slot + 1, 0)
        high = jnp.where(rows & (slot == 5), 1, 2)

        def every(block, carry):
            part(block, False)
            return carry

        lax.fori_loop(low, high, every, 0)

    steps = 2 + jnp.where(row0, 2 * cs, jnp.where(cs >= 2, 3, 2 * cs))

    def slot_of(n):
        m = n - 2
        far = jnp.where(m < 4, 2 + 4 * lax.rem(m, 2) + lax.rem(r + m // 2, 2), 4 + lax.rem(r + m, 2))
        usual = 2 + 2 * (m // 2) + lax.rem(r + m, 2)
        usual = jnp.where(rows & (m == 2), 5, usual)
        return jnp.where(n < 2, n, jnp.where(last_chip, far, usual))

    near_y = y + 1 - 2 * lax.rem(y, 2)
    ring_y = 3 - y
    over_y = lax.rem(y + 2, 4)

    def quarter(ref, q):
        return ref[pl.ds(pl.multiple_of(q * 128, 128), 128), :]

    def first_copy(slot, a):
        return pltpu.make_async_remote_copy(
            src_ref=first_out.at[slot, a], dst_ref=first_in.at[slot, a],
            send_sem=s_first.at[slot, a], recv_sem=r_first.at[slot, a],
            device_id=((near_y, ring_y)[a], b), device_id_type=MESH,
        )

    def second_copy(slot, a):
        return pltpu.make_async_remote_copy(
            src_ref=second_out.at[slot, a], dst_ref=second_in.at[slot, a],
            send_sem=s_second.at[slot, a], recv_sem=r_second.at[slot, a],
            device_id=((ring_y, near_y)[a], b), device_id_type=MESH,
        )

    def last_copy(slot):
        dist = slot // 2
        return copy(
            last_out.at[slot], last_in.at[dist, r], s_last.at[slot], r_last.at[dist, r],
            2 * (c - dist) + lax.rem(slot, 2),
        )

    def first_exchange(slot):
        for a, total, one, two in ((0, dk, near_y, ring_y), (1, dv, ring_y, near_y)):
            first_out[slot, a, 0] = quarter(total, one).astype(BF)
            first_out[slot, a, 1] = quarter(total, over_y).astype(BF)
            first_copy(slot, a).start()
            kept[slot, a, 0] = quarter(total, y)
            kept[slot, a, 1] = quarter(total, two)

    def second_exchange(slot):
        for a in range(2):
            first_copy(slot, a).wait_recv()
            second_out[slot, a] = (kept[slot, a, 1] + first_in[slot, a, 1].astype(F32)).astype(BF)
            second_copy(slot, a).start()
            kept[slot, a, 0] += first_in[slot, a, 0].astype(F32)

    def hand_over(slot):
        for a in range(2):
            second_copy(slot, a).wait_recv()
            kept[slot, a, 0] += second_in[slot, a].astype(F32)

        @pl.when(slot == r)
        def _():
            for a in range(2):
                mine[a] = kept[slot, a, 0]

        @pl.when(slot != r)
        def _():
            for a in range(2):
                last_out[slot, a] = kept[slot, a, 0].astype(BF)
            last_copy(slot).start()

    dq_copy = copy(dq_out, dq_in, s_dq, r_dq, sib)

    def query_gradients():
        for h in range(8):
            o = (h % 2) * 128
            dq_out[:, h * 128 : (h + 1) * 128] = (
                (dqt[sr * 4 + h // 2, :, o : o + 128] * SCALE).T.astype(BF)
            )
        dq_copy.start()
        for h in range(8):
            o = (h % 2) * 128
            cols = pl.ds(pl.multiple_of(r * 1024 + h * 128, 128), 128)
            dq_ref[0, :, cols] = (dqt[r * 4 + h // 2, :, o : o + 128] * SCALE).T.astype(BF)

    kv_wait(sr)
    sends_two = rows & next2 & (r == 1)

    def step(n, carry):
        @pl.when(n < steps)
        def _():
            slot = slot_of(n)

            @pl.when(n >= 2)
            def _():
                kv_wait(slot)

            @pl.when(passes & (slot // 2 == 1))
            def _():
                pass_copy(slot).start()

            tile(slot)
            first_exchange(slot)

        @pl.when((n == 0) & sends_two)
        def _():
            for d in to_chip(2, 5, s_two):
                d.start()

        @pl.when(n == steps)
        def _():
            query_gradients()

        @pl.when((n >= 1) & (n <= steps))
        def _():
            second_exchange(slot_of(n - 1))

        @pl.when(n >= 2)
        def _():
            hand_over(slot_of(n - 2))

        return carry

    lax.fori_loop(0, steps + 2, step, 0)

    dq_copy.wait_recv()
    dq_ref[0, :, pl.ds(pl.multiple_of(sr * 1024, 1024), 1024)] = dq_in[...]

    def last_wait(dist, head):
        copy(
            last_in.at[dist, head], last_in.at[dist, head], s_last.at[0], r_last.at[dist, head], sib
        ).wait_recv()
        mine[...] += last_in[dist, head].astype(F32)

    def finish(head):
        @pl.when(next1)
        def _():
            last_wait(1, head)

        @pl.when(next2 & (row0 | (r == 1)))
        def _():
            last_wait(2, head)

        @pl.when(first_chip)
        def _():
            last_wait(3, head)

        cols = pl.ds(pl.multiple_of(head * 128, 128), 128)
        dk_ref[0, :, cols] = (mine[0] * SCALE).astype(BF)
        dv_ref[0, :, cols] = mine[1].astype(BF)

    finish(r)
    mine[...] = jnp.zeros_like(mine)
    last_wait(0, sr)
    finish(sr)

    for i in range(3):
        swap_copy(i).wait_send()
    own_copy.wait_send()
    dq_copy.wait_send()
    for i in range(1, 4):
        lse_copy(i).wait_send()

    @pl.when(jnp.logical_not(stat_here))
    def _():
        lse_copy(0).wait_send()

    def sent(n, carry):
        slot = slot_of(n)
        for a in range(2):
            first_copy(slot, a).wait_send()
            second_copy(slot, a).wait_send()

        @pl.when(slot != r)
        def _():
            last_copy(slot).wait_send()

        @pl.when(passes & (slot // 2 == 1))
        def _():
            pass_copy(slot).wait_send()

        return carry

    lax.fori_loop(0, steps, sent, 0)

    @pl.when(next1)
    def _():
        for d in to_chip(1, 2 + r, s_next):
            d.wait_send()

    @pl.when(first_chip)
    def _():
        for d in to_chip(3, 6 + r, s_far):
            d.wait_send()

    @pl.when(sends_two)
    def _():
        for d in to_chip(2, 5, s_two):
            d.wait_send()


def fused(queries, keys, values, outputs, output_gradient, log_norms, doc_lengths):
    vmem = pl.BlockSpec(memory_space=pltpu.VMEM)
    dma = pltpu.SemaphoreType.DMA
    return pl.pallas_call(
        kernel,
        out_shape=(
            jax.ShapeDtypeStruct((1, 128, 2048), BF),
            jax.ShapeDtypeStruct((1, 128, 256), BF),
            jax.ShapeDtypeStruct((1, 128, 256), BF),
        ),
        in_specs=[vmem] * 6 + [pl.BlockSpec(memory_space=pltpu.SMEM)],
        out_specs=(vmem, vmem, vmem),
        scratch_shapes=[
            pltpu.VMEM((8, 2, 512, 128), BF),
            pltpu.VMEM((2, 512, 128), BF),
            pltpu.VMEM((8, 2, 2, 128, 128), BF),
            pltpu.VMEM((8, 2, 2, 128, 128), BF),
            pltpu.VMEM((8, 2, 128, 128), BF),
            pltpu.VMEM((8, 2, 128, 128), BF),
            pltpu.VMEM((8, 2, 2, 128, 128), F32),
            pltpu.VMEM((8, 2, 128, 128), BF),
            pltpu.VMEM((4, 2, 2, 128, 128), BF),
            pltpu.VMEM((2, 128, 128), F32),
            pltpu.VMEM((2, 2, 4, 128), F32),
            pltpu.VMEM((3, 128, 1024), BF),
            pltpu.VMEM((128, 1024), BF),
            pltpu.VMEM((128, 1024), BF),
            pltpu.VMEM((8, 256, 128), BF),
            pltpu.VMEM((8, 256, 128), BF),
            pltpu.VMEM((8, 256, 256), BF),
            pltpu.VMEM((8, 256, 256), BF),
            pltpu.VMEM((8, 128, 256), F32),
            pltpu.VMEM((128, 512), BF),
            pltpu.VMEM((512, 128), F32),
            pltpu.VMEM((512, 128), F32),
            pltpu.VMEM((512, 128), BF),
            dma, dma((2,)), dma((2,)), dma((2,)), dma((2,)), dma((8,)),
            dma((8, 2)), dma((8, 2)), dma((8, 2)), dma((8, 2)), dma((8,)), dma((4, 2)),
            dma((4,)), dma((2, 2)), dma((3,)), dma((3,)), dma, dma,
        ],
        compiler_params=pltpu.CompilerParams(
            collective_id=0, has_side_effects=True, vmem_limit_bytes=56 * 2**20
        ),
    )(queries, keys, values, outputs, output_gradient, log_norms, doc_lengths)


def passed_along(x, axis, by):
    peers = lax.axis_size(axis)
    return lax.ppermute(x, axis, [(i, (i + by) % peers) for i in range(peers)])


def shifted(block, axis, distance):
    devices = range(lax.axis_size(axis))
    route = [(i - distance, i) for i in devices if i - distance in devices]
    return lax.ppermute(block, axis, route)


def doc_starts(doc_lengths, positions):
    firsts = jnp.cumsum(doc_lengths) - doc_lengths
    return jnp.max(jnp.where(firsts[None, :] <= positions[:, None], firsts[None, :], 0), axis=1)


def pass_grads(key_gradient_total, total_value_gradient):
    return passed_along((key_gradient_total, total_value_gradient), "blk", 1)


def scattered_sum(x):
    parts = x.reshape(4, x.shape[0] // 4, x.shape[1])
    return jnp.sum(lax.all_to_all(parts, "head", split_axis=0, concat_axis=0), axis=0)


def ring(queries, keys, values, outputs, output_gradient, log_norms, doc_lengths):
    block_count = lax.axis_size("blk")
    block_index = lax.axis_index("blk")
    every_query, every_output, grad_all = (
        lax.all_to_all(queries, "head", split_axis=2, concat_axis=1, tiled=True),
        lax.all_to_all(outputs, "head", split_axis=2, concat_axis=1, tiled=True),
        lax.all_to_all(output_gradient, "head", split_axis=2, concat_axis=1, tiled=True),
    )
    rows_per_block = every_query.shape[1]
    head_features = keys.shape[2] // KEY_VALUE_HEADS
    local_heads = every_query.shape[2] // head_features
    query_group_size = QUERY_HEADS // KEY_VALUE_HEADS
    logit_scale = head_features ** (-0.5)
    query_loc = every_query[0].reshape(rows_per_block, local_heads, head_features)
    grad_loc = grad_all[0].reshape(rows_per_block, local_heads, head_features)
    output_loc = every_output[0].reshape(rows_per_block, local_heads, head_features)
    row_delta = jnp.sum(grad_loc.astype(jnp.float32) * output_loc.astype(jnp.float32), axis=-1).T
    row_statistics = log_norms[0]
    kv_head = lax.axis_index("head") * local_heads // query_group_size
    key_own = lax.dynamic_slice_in_dim(keys[0], kv_head * head_features, head_features, 1)
    value_own = lax.dynamic_slice_in_dim(values[0], kv_head * head_features, head_features, 1)
    query_pos = block_index * rows_per_block + jnp.arange(rows_per_block, dtype=jnp.int32)
    first_pos = doc_starts(doc_lengths, query_pos)

    def tile_grads(pair, key_block):
        key_blk, value_blk = pair
        key_pos = key_block * rows_per_block + jnp.arange(rows_per_block, dtype=jnp.int32)
        allowed = (key_pos[None, :] <= query_pos[:, None]) & (
            key_pos[None, :] >= first_pos[:, None]
        )
        scores = logit_scale * jnp.einsum(
            "qhd,kd->hqk", query_loc, key_blk, preferred_element_type=jnp.float32
        )
        probability = jnp.where(allowed[None], jnp.exp(scores - row_statistics[:, :, None]), 0.0)
        prob_low = probability.astype(jnp.bfloat16)
        value_add = jnp.einsum(
            "hqk,qhd->kd", prob_low, grad_loc, preferred_element_type=jnp.float32
        )
        dprob = jnp.einsum("qhd,kd->hqk", grad_loc, value_blk, preferred_element_type=jnp.float32)
        dscore = (probability * (dprob - row_delta[:, :, None])).astype(jnp.bfloat16)
        query_add = jnp.einsum("hqk,kd->qhd", dscore, key_blk, preferred_element_type=jnp.float32)
        key_increment = jnp.einsum(
            "hqk,qhd->kd", dscore, query_loc, preferred_element_type=jnp.float32
        )
        return (query_add, key_increment, value_add)

    def no_grads():
        flat = jnp.zeros((rows_per_block, head_features), jnp.float32)
        return (jnp.zeros((rows_per_block, local_heads, head_features), jnp.float32), flat, flat)

    def visit_block(carry_state, cycle_step):
        pair, query_acc, key_gradient_total, total_value_gradient = carry_state
        key_block = (block_index - cycle_step) % block_count
        active = (key_block <= block_index) & ((key_block + 1) * rows_per_block - 1 >= first_pos[0])
        query_add, key_increment, value_add = lax.cond(
            active, lambda: tile_grads(pair, key_block), no_grads
        )
        return (
            pair,
            query_acc + query_add,
            key_gradient_total + key_increment,
            total_value_gradient + value_add,
        )

    def cycle_turn(cycle_step, carry_state):
        pair, query_acc, key_gradient_total, total_value_gradient = visit_block(
            carry_state, cycle_step
        )
        pair = shifted((pair[0], pair[1]), "blk", 1)
        key_gradient_total, total_value_gradient = pass_grads(
            key_gradient_total, total_value_gradient
        )
        return (pair, query_acc, key_gradient_total, total_value_gradient)

    flat_zero = jnp.zeros((rows_per_block, head_features), jnp.float32)
    initial = (
        (key_own, value_own),
        jnp.zeros((rows_per_block, local_heads, head_features), jnp.float32),
        flat_zero,
        flat_zero,
    )
    carry_state = lax.fori_loop(0, block_count - 1, cycle_turn, initial)
    pair, query_acc, key_gradient_total, total_value_gradient = visit_block(
        carry_state, block_count - 1
    )
    key_gradient_total, total_value_gradient = pass_grads(key_gradient_total, total_value_gradient)
    broad_zeros = jnp.zeros((rows_per_block, KEY_VALUE_HEADS * head_features), jnp.float32)
    key_broadcast = lax.dynamic_update_slice_in_dim(
        broad_zeros, key_gradient_total, kv_head * head_features, 1
    )
    value_wide = lax.dynamic_update_slice_in_dim(
        broad_zeros, total_value_gradient, kv_head * head_features, 1
    )
    key_part, value_part = scattered_sum(key_broadcast), scattered_sum(value_wide)
    keys_gradient = (logit_scale * key_part).astype(jnp.bfloat16)[None]
    values_gradient = value_part.astype(jnp.bfloat16)[None]
    query_out = (
        (logit_scale * query_acc)
        .astype(jnp.bfloat16)
        .reshape(1, rows_per_block, local_heads * head_features)
    )
    query_grad = lax.all_to_all(query_out, "head", split_axis=1, concat_axis=2, tiled=True)
    return (query_grad, keys_gradient, values_gradient)


def shards(*arrays):
    short = jnp.max(arrays[-1][1:]) <= 1537
    return lax.cond(short, fused, ring, *arrays)


def solution(mesh):
    in_specs = (
        P("blk", "head", None),
        P("blk", None, None),
        P("blk", None, None),
        P("blk", "head", None),
        P("blk", "head", None),
        P("blk", "head", None),
        P(),
    )
    out_specs = (P("blk", "head", None), P("blk", "head", None), P("blk", "head", None))
    return jax.shard_map(shards, mesh=mesh, in_specs=in_specs, out_specs=out_specs, check_vma=False)
```

```python
import functools

import jax
import jax.numpy as jnp
from jax import lax
from jax.experimental import pallas as pl
from jax.experimental.pallas import tpu as pltpu
from jax.sharding import PartitionSpec as P

QUERY_HEADS = 16
KEY_VALUE_HEADS = 2
BF = jnp.bfloat16
F32 = jnp.float32
SCALE = 128**-0.5
EXP2_SCALE = SCALE * 1.4426950408889634
FAR = 16384.0
MESH = pl.DeviceIdType.MESH


def split3(x):
    hi = x.astype(BF).astype(F32)
    rest = x - hi
    mid = rest.astype(BF).astype(F32)
    return hi, mid, rest - mid


def kernel(
    q_ref, k_ref, v_ref, o_ref, g_ref, lse_ref, len_ref,
    dq_ref, dk_ref, dv_ref,
    kvs, other, first_out, first_in, second_out, second_in, kept, last_out, last_in, direct_out, direct_in, mine,
    lse_all, here, swap, dq_out, dq_in,
    qn, gn, qta, gta, dqt, kt, dk, dv, aug,
    s_load, s_rows, s_own, r_own, s_x, r_x, s_spread, r_spread, s_relay, r_relay,
    s_first, r_first, s_second, r_second, s_last, r_last, s_direct, r_direct,
    s_lse, r_lse, s_swap, r_swap, s_dq, r_dq,
):
    y = lax.axis_index("head")
    b = lax.axis_index("blk")
    r = lax.rem(b, 2)
    sr = 1 - r
    c = b // 2
    row0 = b < 8
    rows = b >= 8
    cs = jnp.where(row0, c, c - 4)
    last = jnp.where(row0, 3, 27)
    prev1, next1 = cs >= 1, cs <= last - 1
    prev2, next2 = cs >= 2, cs <= last - 2
    first_chip = row0 & (cs == 0)
    last_chip = row0 & (cs == 3)
    second_chip = row0 & (cs == 1)
    sib = 2 * c + sr

    def copy(src, dst, send, recv, blk):
        return pltpu.make_async_remote_copy(
            src_ref=src, dst_ref=dst, send_sem=send, recv_sem=recv,
            device_id={"blk": blk}, device_id_type=MESH,
        )

    def head_cols(head, width):
        return pl.ds(pl.multiple_of(head * width, 128), width)

    loads = [
        pltpu.make_async_copy(ref.at[0, :, head_cols(head, 128)], dst.at[i], s_load.at[i, k])
        for k, (head, dst) in enumerate(((r, kvs.at[r]), (sr, other)))
        for i, ref in enumerate((k_ref, v_ref))
    ]
    row_loads = [
        pltpu.make_async_copy(ref.at[0, :, head_cols(r, 1024)], here.at[i], s_rows.at[i])
        for i, ref in enumerate((q_ref, g_ref, o_ref))
    ]
    for d in loads + row_loads:
        d.start()

    barrier = pltpu.get_barrier_semaphore()

    def greet(cond, blk):
        @pl.when(cond)
        def _():
            for core in range(2):
                pl.semaphore_signal(
                    barrier, inc=1, device_id={"blk": blk + core}, device_id_type=MESH
                )

        return jnp.where(cond, 2, 0)

    def greet_all(cond, blk):
        @pl.when(cond)
        def _():
            for i in range(8):
                pl.semaphore_signal(
                    barrier, inc=1, device_id=(i // 2, blk + i % 2), device_id_type=MESH
                )

        return jnp.where(cond, 8, 0)

    pl.semaphore_signal(barrier, inc=1, device_id={"blk": sib}, device_id_type=MESH)
    partners = 1 + greet(prev1, 2 * c - 2)
    partners += greet(next1, 2 * c + 2)
    partners += greet(prev2 & jnp.logical_not(last_chip), 2 * c - 4)
    partners += greet(next2 & jnp.logical_not(second_chip), 2 * c + 4)
    partners += greet_all(last_chip, 2 * c - 4)
    partners += greet_all(second_chip, 2 * c + 4)
    partners += greet(first_chip, 2 * c + 6)
    partners += greet(last_chip, 2 * c - 6)
    for i in range(1, 4):
        for core in range(2):
            pl.semaphore_signal(
                barrier, inc=1, device_id=(lax.rem(y + i, 4), 2 * c + core), device_id_type=MESH
            )
    pl.semaphore_wait(barrier, partners + 6)

    near_y = y + 1 - 2 * lax.rem(y, 2)
    ring_y = 3 - y
    over_y = lax.rem(y + 2, 4)

    def rows_of(q):
        return pl.ds(pl.multiple_of(q * 128, 128), 128)

    def to_chip(dist, slot, which):
        own, far, dst = kvs.at[r], other, kvs.at[slot]
        if dist == 2:
            own, far, dst = (x.at[:, rows_of(y)] for x in (own, far, dst))
        core = (r, sr)[which]
        return copy(
            (own, far)[which], dst, s_x.at[dist - 1, which], r_x.at[slot], 2 * (c + dist) + core
        )

    own_copy = copy(other, kvs.at[r], s_own, r_own, sib)

    def spread_copy(slot, a):
        part = kvs.at[slot, :, rows_of(y)]
        return pltpu.make_async_remote_copy(
            src_ref=part, dst_ref=part,
            send_sem=s_spread.at[slot, a], recv_sem=r_spread.at[slot, a],
            device_id=((near_y, ring_y)[a], b), device_id_type=MESH,
        )

    def spread_wait(slot, a):
        part = kvs.at[slot, :, rows_of((near_y, ring_y)[a])]
        pltpu.make_async_remote_copy(
            src_ref=part, dst_ref=part,
            send_sem=s_spread.at[slot, a], recv_sem=r_spread.at[slot, a],
            device_id=((near_y, ring_y)[a], b), device_id_type=MESH,
        ).wait_recv()

    def relay_copy(slot, a):
        part = kvs.at[slot, a, rows_of((ring_y, near_y)[a])]
        return pltpu.make_async_remote_copy(
            src_ref=part, dst_ref=part,
            send_sem=s_relay.at[slot, a], recv_sem=r_relay.at[slot, a],
            device_id=((near_y, ring_y)[a], b), device_id_type=MESH,
        )

    def relay_wait(slot, a):
        part = kvs.at[slot, a, rows_of(over_y)]
        pltpu.make_async_remote_copy(
            src_ref=part, dst_ref=part,
            send_sem=s_relay.at[slot, a], recv_sem=r_relay.at[slot, a],
            device_id=((near_y, ring_y)[a], b), device_id_type=MESH,
        ).wait_recv()

    def spread(slot):
        part = kvs.at[slot, :, rows_of(y)]
        copy(part, part, s_own, r_x.at[slot], sib).wait_recv()
        for a in range(2):
            spread_copy(slot, a).start()

    def relay(slot):
        for a in range(2):
            spread_wait(slot, 1 - a)
            relay_copy(slot, a).start()

    def swap_copy(i):
        src = (q_ref, g_ref, o_ref)[i]
        return copy(src.at[0, :, head_cols(sr, 1024)], swap.at[i], s_swap.at[i], r_swap.at[i], sib)

    stat_core = y // 2
    stat_here = r == stat_core

    def lse_tokens(peer):
        return lse_ref.at[0, :, pl.ds(pl.multiple_of(peer * 128, 128), 128)]

    def lse_copy(i):
        peer = lax.rem(y + i, 4)
        return pltpu.make_async_remote_copy(
            src_ref=lse_tokens(peer), dst_ref=lse_all.at[r, lax.rem(y, 2)],
            send_sem=s_lse.at[i], recv_sem=r_lse.at[r, lax.rem(y, 2)],
            device_id=(peer, 2 * c + stat_core), device_id_type=MESH,
        )

    sends_two = next2 & (row0 | (r == 1))

    def to_chips(act):
        def at(cond, dist, slot, which):
            @pl.when(cond)
            def _():
                act(to_chip(dist, slot, which))

        at(next1, 1, 2 + r, 0)
        at(first_chip, 3, 6 + r, 0)
        at(sends_two, 2, 4 + r, 0)
        at(sends_two, 2, 4 + r, 1)
        at(next1, 1, 2 + r, 1)
        at(first_chip, 3, 6 + r, 1)

    for i in range(3):
        swap_copy(i).start()
    for d in loads:
        d.wait()
    own_copy.start()
    to_chips(lambda d: d.start())
    for i in range(1, 4):
        lse_copy(i).start()

    @pl.when(stat_here)
    def _():
        mine_too = pltpu.make_async_copy(lse_tokens(y), lse_all.at[r, lax.rem(y, 2)], s_lse.at[0])
        mine_too.start()
        mine_too.wait()

    @pl.when(jnp.logical_not(stat_here))
    def _():
        lse_copy(0).start()

    lane = lax.broadcasted_iota(jnp.int32, (8, 128), 1)
    row = lax.broadcasted_iota(jnp.int32, (32, 128), 0)
    lo_l = jnp.zeros((8, 128), jnp.int32)
    len_l = jnp.zeros((8, 128), jnp.int32)
    lo_r = jnp.zeros((32, 128), jnp.int32)
    len_r = jnp.zeros((32, 128), jnp.int32)
    for i in range(32):
        n = len_ref[i]
        lo_l += jnp.where(lane > i, n, 0)
        len_l += jnp.where(lane == i, n, 0)
        lo_r += jnp.where(row > i, n, 0)
        len_r += jnp.where(row == i, n, 0)
    hi_l = lo_l + len_l
    aug_row = lax.broadcasted_iota(jnp.int32, (128, 128), 0)

    def prepare(block, q_of, g_of, o_of):
        for h in range(8):
            ch, o = block * 4 + h // 2, (h % 2) * 128
            qh, gh, oh = q_of(h), g_of(h), o_of(h)
            gt = gh.T
            qn[ch, o : o + 128, :] = qh
            gn[ch, o : o + 128, :] = gh
            qta[ch, 0:128, o : o + 128] = qh.T
            gta[ch, 0:128, o : o + 128] = gt
            delta = jnp.sum(gt.astype(F32) * oh.T.astype(F32), axis=0, keepdims=True)
            d0, d1, d2 = split3(-delta)
            extra = jnp.where(aug_row == 32, d0, 0.0)
            extra = jnp.where(aug_row == 33, d1, extra)
            extra = jnp.where(aug_row == 34, d2, extra)
            gta[ch, 128:256, o : o + 128] = extra.astype(BF)

    def prepare_stats(block):
        qpos = (2 * c + block) * 512 + y * 128 + lax.broadcasted_iota(jnp.int32, (32, 128), 1)
        doc_rows = jnp.where((qpos >= lo_r) & (qpos < lo_r + len_r), 0.0, -FAR)
        doc_rows = jnp.concatenate([doc_rows, jnp.zeros((96, 128), F32)], 0)
        for h in range(8):
            ch, o = block * 4 + h // 2, (h % 2) * 128
            stat = lse_all[block, h // 4, h % 4 : h % 4 + 1, :] * (-(128.0**0.5))
            d0, d1, d2 = split3(stat)
            extra = jnp.where(aug_row == 32, d0, doc_rows)
            extra = jnp.where(aug_row == 33, d1, extra)
            extra = jnp.where(aug_row == 34, d2, extra)
            qta[ch, 128:256, o : o + 128] = extra.astype(BF)

    def rows_in(ref):
        return [lambda h, i=i: ref[i, :, h * 128 : (h + 1) * 128] for i in range(3)]

    def lse_wait(block, half):
        @pl.when(jnp.logical_not((block == r) & (y == 2 * r + half)))
        def _():
            pltpu.make_async_remote_copy(
                src_ref=lse_all.at[block, half], dst_ref=lse_all.at[block, half],
                send_sem=s_lse.at[0], recv_sem=r_lse.at[block, half],
                device_id=(y, sib), device_id_type=MESH,
            ).wait_recv()

    dqt[...] = jnp.zeros_like(dqt)
    for d in row_loads:
        d.wait()
    prepare(r, *rows_in(here))
    for i in range(3):
        swap_copy(i).wait_recv()
    prepare(sr, *rows_in(swap))
    for block in range(2):
        for half in range(2):
            lse_wait(block, half)
        prepare_stats(block)

    def tile(slot):
        lane_k = lax.broadcasted_iota(jnp.int32, (512, 128), 1)
        kpos = (2 * (c - slot // 2) + lax.rem(slot, 2)) * 512
        kpos = kpos + lax.broadcasted_iota(jnp.int32, (512, 128), 0)
        inside = (kpos >= lo_l[0:1]) & (kpos < hi_l[0:1])
        ones = (lane_k >= 32) & (lane_k < 35)
        aug[...] = jnp.where(inside | ones, 1.0, 0.0).astype(BF)
        kt[...] = kvs[slot, 0].T
        whole = (slot >= 2) & jnp.logical_not(rows & (slot == 5))

        def scores(kj, vj, ch, causal):
            st = jnp.dot(kj, qta[ch], preferred_element_type=F32)
            p = jnp.exp2(st * EXP2_SCALE)
            if causal:
                krow = lax.broadcasted_iota(jnp.int32, (512, 256), 0)
                qcol = lax.broadcasted_iota(jnp.int32, (512, 256), 1) & 127
                p = jnp.where(krow <= qcol + y * 128, p, 0.0)
            dp = jnp.dot(vj, gta[ch], preferred_element_type=F32)
            return p.astype(BF), (p * dp).astype(BF)

        def gradients(pair, ch, first):
            dvi = jnp.dot(pair[0], gn[ch], preferred_element_type=F32)
            dki = jnp.dot(pair[1], qn[ch], preferred_element_type=F32)
            if first:
                dv[...] = dvi
                dk[...] = dki
            else:
                dv[...] += dvi
                dk[...] += dki
            dqt[ch] += jnp.dot(kt[...], pair[1], preferred_element_type=F32)

        def part(chunks, causal, first):
            kj = jnp.concatenate([kvs[slot, 0], aug[...]], 1)
            vj = jnp.concatenate([kvs[slot, 1], aug[...]], 1)
            pair = scores(kj, vj, chunks[0], causal)
            for i, ch in enumerate(chunks):
                later = scores(kj, vj, chunks[i + 1], causal) if i + 1 < len(chunks) else None
                gradients(pair, ch, first and i == 0)
                pair = later

        @pl.when(whole)
        def _():
            part(range(8), False, True)

        @pl.when(jnp.logical_not(whole))
        def _():
            dk[...] = jnp.zeros_like(dk)
            dv[...] = jnp.zeros_like(dv)

            @pl.when(slot < 2)
            def _():
                part([slot * 4 + i for i in range(4)], True, False)

            @pl.when(slot != 1)
            def _():
                block = jnp.where(slot == 0, 1, 0)
                part([block * 4 + i for i in range(4)], False, False)

    steps = 2 + jnp.where(row0, 2 * cs, jnp.where(cs >= 2, 3, 2 * cs))

    def slot_of(n):
        m = n - 2
        far = jnp.where(m < 4, 2 + 4 * lax.rem(m, 2) + lax.rem(r + m // 2, 2), 4 + lax.rem(r + m, 2))
        usual = 2 + 2 * (m // 2) + lax.rem(r + m, 2)
        usual = jnp.where(rows & (m == 2), 5, usual)
        return jnp.where(n < 2, n, jnp.where(last_chip, far, usual))

    def quarter(ref, q):
        return ref[rows_of(q), :]

    def first_copy(slot, a):
        return pltpu.make_async_remote_copy(
            src_ref=first_out.at[slot, a], dst_ref=first_in.at[slot, a],
            send_sem=s_first.at[slot, a], recv_sem=r_first.at[slot, a],
            device_id=((near_y, ring_y)[a], b), device_id_type=MESH,
        )

    def second_copy(slot, a):
        return pltpu.make_async_remote_copy(
            src_ref=second_out.at[slot, a], dst_ref=second_in.at[slot, a],
            send_sem=s_second.at[slot, a], recv_sem=r_second.at[slot, a],
            device_id=((ring_y, near_y)[a], b), device_id_type=MESH,
        )

    def last_copy(slot):
        dist = slot // 2
        return copy(
            last_out.at[slot], last_in.at[dist, r], s_last.at[slot], r_last.at[dist, r],
            2 * (c - dist) + lax.rem(slot, 2),
        )

    def first_exchange(slot):
        for a, total, one, two in ((0, dk, near_y, ring_y), (1, dv, ring_y, near_y)):
            first_out[slot, a, 0] = quarter(total, one).astype(BF)
            first_out[slot, a, 1] = quarter(total, over_y).astype(BF)
            first_copy(slot, a).start()
            kept[slot, a, 0] = quarter(total, y)
            kept[slot, a, 1] = quarter(total, two)

    def goes_direct(slot):
        return last_chip & (slot == 4 + sr)

    def direct_copy(slot, i):
        p, q = lax.rem(slot, 2), lax.rem(y + i, 4)
        return pltpu.make_async_remote_copy(
            src_ref=direct_out.at[p, i], dst_ref=direct_in.at[r, i],
            send_sem=s_direct.at[p, i], recv_sem=r_direct.at[r, i],
            device_id=(q, 2 * (c - 2) + p), device_id_type=MESH,
        )

    def direct(slot):
        p = lax.rem(slot, 2)
        for i in range(4):
            q = lax.rem(y + i, 4)
            direct_out[p, i, 0] = quarter(dk, q).astype(BF)
            direct_out[p, i, 1] = quarter(dv, q).astype(BF)
            direct_copy(slot, i).start()

    def second_exchange(slot):
        for a in range(2):
            first_copy(slot, a).wait_recv()
            second_out[slot, a] = (kept[slot, a, 1] + first_in[slot, a, 1].astype(F32)).astype(BF)
            second_copy(slot, a).start()
            kept[slot, a, 0] += first_in[slot, a, 0].astype(F32)

    def hand_over(slot):
        for a in range(2):
            second_copy(slot, a).wait_recv()
            kept[slot, a, 0] += second_in[slot, a].astype(F32)

        @pl.when(slot == r)
        def _():
            for a in range(2):
                mine[a] = kept[slot, a, 0]

        @pl.when(slot != r)
        def _():
            for a in range(2):
                last_out[slot, a] = kept[slot, a, 0].astype(BF)
            last_copy(slot).start()

    dq_copy = copy(dq_out, dq_in, s_dq, r_dq, sib)

    def query_gradients():
        for h in range(8):
            o = (h % 2) * 128
            dq_out[:, h * 128 : (h + 1) * 128] = (
                (dqt[sr * 4 + h // 2, :, o : o + 128] * SCALE).T.astype(BF)
            )
        dq_copy.start()
        for h in range(8):
            o = (h % 2) * 128
            cols = pl.ds(pl.multiple_of(r * 1024 + h * 128, 128), 128)
            dq_ref[0, :, cols] = (dqt[r * 4 + h // 2, :, o : o + 128] * SCALE).T.astype(BF)

    copy(kvs.at[sr], kvs.at[sr], s_own, r_own, sib).wait_recv()

    def step(n, carry):
        @pl.when(n < steps)
        def _():
            slot = slot_of(n)

            @pl.when((n >= 2) & (slot // 2 == 2))
            def _():
                for a in range(2):
                    relay_wait(slot, a)

            @pl.when((n >= 2) & (slot // 2 != 2))
            def _():
                copy(kvs.at[slot], kvs.at[slot], s_own, r_x.at[slot], sib).wait_recv()

            tile(slot)

            @pl.when(goes_direct(slot))
            def _():
                direct(slot)

            @pl.when(jnp.logical_not(goes_direct(slot)))
            def _():
                first_exchange(slot)

        @pl.when((n == jnp.where(last_chip, 2, 1)) & prev2)
        def _():
            spread(5)

            @pl.when(row0)
            def _():
                spread(4)

        @pl.when((n == jnp.where(last_chip, 4, 2)) & prev2)
        def _():
            relay(5)

            @pl.when(row0)
            def _():
                relay(4)

        @pl.when(n == steps)
        def _():
            query_gradients()

        @pl.when((n >= 2) & (n <= steps + 1))
        def _():
            slot = slot_of(n - 2)

            @pl.when(jnp.logical_not(goes_direct(slot)))
            def _():
                second_exchange(slot)

        @pl.when(n >= 4)
        def _():
            slot = slot_of(n - 4)

            @pl.when(jnp.logical_not(goes_direct(slot)))
            def _():
                hand_over(slot)

        return carry

    lax.fori_loop(0, steps + 4, step, 0)

    dq_copy.wait_recv()
    dq_ref[0, :, pl.ds(pl.multiple_of(sr * 1024, 1024), 1024)] = dq_in[...]

    def last_wait(dist, head):
        copy(
            last_in.at[dist, head], last_in.at[dist, head], s_last.at[0], r_last.at[dist, head], sib
        ).wait_recv()
        mine[...] += last_in[dist, head].astype(F32)

    def finish(head):
        @pl.when(next1)
        def _():
            last_wait(1, head)

        straight = second_chip & (head == sr)

        @pl.when(sends_two & jnp.logical_not(straight))
        def _():
            last_wait(2, head)

        @pl.when(straight)
        def _():
            for i in range(4):
                copy(
                    direct_in.at[head, i], direct_in.at[head, i], s_own, r_direct.at[head, i], sib
                ).wait_recv()
                mine[...] += direct_in[head, i].astype(F32)

        @pl.when(first_chip)
        def _():
            last_wait(3, head)

        cols = pl.ds(pl.multiple_of(head * 128, 128), 128)
        dk_ref[0, :, cols] = (mine[0] * SCALE).astype(BF)
        dv_ref[0, :, cols] = mine[1].astype(BF)

    finish(r)
    mine[...] = jnp.zeros_like(mine)
    last_wait(0, sr)
    finish(sr)

    for i in range(3):
        swap_copy(i).wait_send()
    own_copy.wait_send()
    dq_copy.wait_send()
    for i in range(1, 4):
        lse_copy(i).wait_send()

    @pl.when(jnp.logical_not(stat_here))
    def _():
        lse_copy(0).wait_send()

    def sent(n, carry):
        slot = slot_of(n)

        @pl.when(goes_direct(slot))
        def _():
            for i in range(4):
                direct_copy(slot, i).wait_send()

        @pl.when(jnp.logical_not(goes_direct(slot)))
        def _():
            for a in range(2):
                first_copy(slot, a).wait_send()
                second_copy(slot, a).wait_send()

        @pl.when((slot != r) & jnp.logical_not(goes_direct(slot)))
        def _():
            last_copy(slot).wait_send()

        @pl.when((n >= 2) & (slot // 2 == 2))
        def _():
            for a in range(2):
                spread_copy(slot, a).wait_send()
                relay_copy(slot, a).wait_send()

        return carry

    lax.fori_loop(0, steps, sent, 0)

    to_chips(lambda d: d.wait_send())


def fused(queries, keys, values, outputs, output_gradient, log_norms, doc_lengths):
    vmem = pl.BlockSpec(memory_space=pltpu.VMEM)
    dma = pltpu.SemaphoreType.DMA
    return pl.pallas_call(
        kernel,
        out_shape=(
            jax.ShapeDtypeStruct((1, 128, 2048), BF),
            jax.ShapeDtypeStruct((1, 128, 256), BF),
            jax.ShapeDtypeStruct((1, 128, 256), BF),
        ),
        in_specs=[pl.BlockSpec(memory_space=pl.ANY)] * 6 + [pl.BlockSpec(memory_space=pltpu.SMEM)],
        out_specs=(vmem, vmem, vmem),
        scratch_shapes=[
            pltpu.VMEM((8, 2, 512, 128), BF),
            pltpu.VMEM((2, 512, 128), BF),
            pltpu.VMEM((8, 2, 2, 128, 128), BF),
            pltpu.VMEM((8, 2, 2, 128, 128), BF),
            pltpu.VMEM((8, 2, 128, 128), BF),
            pltpu.VMEM((8, 2, 128, 128), BF),
            pltpu.VMEM((8, 2, 2, 128, 128), F32),
            pltpu.VMEM((8, 2, 128, 128), BF),
            pltpu.VMEM((4, 2, 2, 128, 128), BF),
            pltpu.VMEM((2, 4, 2, 128, 128), BF),
            pltpu.VMEM((2, 4, 2, 128, 128), BF),
            pltpu.VMEM((2, 128, 128), F32),
            pltpu.VMEM((2, 2, 4, 128), F32),
            pltpu.VMEM((3, 128, 1024), BF),
            pltpu.VMEM((3, 128, 1024), BF),
            pltpu.VMEM((128, 1024), BF),
            pltpu.VMEM((128, 1024), BF),
            pltpu.VMEM((8, 256, 128), BF),
            pltpu.VMEM((8, 256, 128), BF),
            pltpu.VMEM((8, 256, 256), BF),
            pltpu.VMEM((8, 256, 256), BF),
            pltpu.VMEM((8, 128, 256), F32),
            pltpu.VMEM((128, 512), BF),
            pltpu.VMEM((512, 128), F32),
            pltpu.VMEM((512, 128), F32),
            pltpu.VMEM((512, 128), BF),
            dma((2, 2)), dma((3,)), dma, dma, dma((3, 2)), dma((8,)), dma((8, 2)), dma((8, 2)), dma((8, 2)), dma((8, 2)),
            dma((8, 2)), dma((8, 2)), dma((8, 2)), dma((8, 2)), dma((8,)), dma((4, 2)), dma((2, 4)), dma((2, 4)),
            dma((4,)), dma((2, 2)), dma((3,)), dma((3,)), dma, dma,
        ],
        compiler_params=pltpu.CompilerParams(
            collective_id=0, has_side_effects=True, vmem_limit_bytes=56 * 2**20
        ),
    )(queries, keys, values, outputs, output_gradient, log_norms, doc_lengths)


def passed_along(x, axis, by):
    peers = lax.axis_size(axis)
    return lax.ppermute(x, axis, [(i, (i + by) % peers) for i in range(peers)])


def shifted(block, axis, distance):
    devices = range(lax.axis_size(axis))
    route = [(i - distance, i) for i in devices if i - distance in devices]
    return lax.ppermute(block, axis, route)


def doc_starts(doc_lengths, positions):
    firsts = jnp.cumsum(doc_lengths) - doc_lengths
    return jnp.max(jnp.where(firsts[None, :] <= positions[:, None], firsts[None, :], 0), axis=1)


def pass_grads(key_gradient_total, total_value_gradient):
    return passed_along((key_gradient_total, total_value_gradient), "blk", 1)


def scattered_sum(x):
    parts = x.reshape(4, x.shape[0] // 4, x.shape[1])
    return jnp.sum(lax.all_to_all(parts, "head", split_axis=0, concat_axis=0), axis=0)


def ring(queries, keys, values, outputs, output_gradient, log_norms, doc_lengths):
    block_count = lax.axis_size("blk")
    block_index = lax.axis_index("blk")
    every_query, every_output, grad_all = (
        lax.all_to_all(queries, "head", split_axis=2, concat_axis=1, tiled=True),
        lax.all_to_all(outputs, "head", split_axis=2, concat_axis=1, tiled=True),
        lax.all_to_all(output_gradient, "head", split_axis=2, concat_axis=1, tiled=True),
    )
    rows_per_block = every_query.shape[1]
    head_features = keys.shape[2] // KEY_VALUE_HEADS
    local_heads = every_query.shape[2] // head_features
    query_group_size = QUERY_HEADS // KEY_VALUE_HEADS
    logit_scale = head_features ** (-0.5)
    query_loc = every_query[0].reshape(rows_per_block, local_heads, head_features)
    grad_loc = grad_all[0].reshape(rows_per_block, local_heads, head_features)
    output_loc = every_output[0].reshape(rows_per_block, local_heads, head_features)
    row_delta = jnp.sum(grad_loc.astype(jnp.float32) * output_loc.astype(jnp.float32), axis=-1).T
    row_statistics = log_norms[0]
    kv_head = lax.axis_index("head") * local_heads // query_group_size
    key_own = lax.dynamic_slice_in_dim(keys[0], kv_head * head_features, head_features, 1)
    value_own = lax.dynamic_slice_in_dim(values[0], kv_head * head_features, head_features, 1)
    query_pos = block_index * rows_per_block + jnp.arange(rows_per_block, dtype=jnp.int32)
    first_pos = doc_starts(doc_lengths, query_pos)

    def tile_grads(pair, key_block):
        key_blk, value_blk = pair
        key_pos = key_block * rows_per_block + jnp.arange(rows_per_block, dtype=jnp.int32)
        allowed = (key_pos[None, :] <= query_pos[:, None]) & (
            key_pos[None, :] >= first_pos[:, None]
        )
        scores = logit_scale * jnp.einsum(
            "qhd,kd->hqk", query_loc, key_blk, preferred_element_type=jnp.float32
        )
        probability = jnp.where(allowed[None], jnp.exp(scores - row_statistics[:, :, None]), 0.0)
        prob_low = probability.astype(jnp.bfloat16)
        value_add = jnp.einsum(
            "hqk,qhd->kd", prob_low, grad_loc, preferred_element_type=jnp.float32
        )
        dprob = jnp.einsum("qhd,kd->hqk", grad_loc, value_blk, preferred_element_type=jnp.float32)
        dscore = (probability * (dprob - row_delta[:, :, None])).astype(jnp.bfloat16)
        query_add = jnp.einsum("hqk,kd->qhd", dscore, key_blk, preferred_element_type=jnp.float32)
        key_increment = jnp.einsum(
            "hqk,qhd->kd", dscore, query_loc, preferred_element_type=jnp.float32
        )
        return (query_add, key_increment, value_add)

    def no_grads():
        flat = jnp.zeros((rows_per_block, head_features), jnp.float32)
        return (jnp.zeros((rows_per_block, local_heads, head_features), jnp.float32), flat, flat)

    def visit_block(carry_state, cycle_step):
        pair, query_acc, key_gradient_total, total_value_gradient = carry_state
        key_block = (block_index - cycle_step) % block_count
        active = (key_block <= block_index) & ((key_block + 1) * rows_per_block - 1 >= first_pos[0])
        query_add, key_increment, value_add = lax.cond(
            active, lambda: tile_grads(pair, key_block), no_grads
        )
        return (
            pair,
            query_acc + query_add,
            key_gradient_total + key_increment,
            total_value_gradient + value_add,
        )

    def cycle_turn(cycle_step, carry_state):
        pair, query_acc, key_gradient_total, total_value_gradient = visit_block(
            carry_state, cycle_step
        )
        pair = shifted((pair[0], pair[1]), "blk", 1)
        key_gradient_total, total_value_gradient = pass_grads(
            key_gradient_total, total_value_gradient
        )
        return (pair, query_acc, key_gradient_total, total_value_gradient)

    flat_zero = jnp.zeros((rows_per_block, head_features), jnp.float32)
    initial = (
        (key_own, value_own),
        jnp.zeros((rows_per_block, local_heads, head_features), jnp.float32),
        flat_zero,
        flat_zero,
    )
    carry_state = lax.fori_loop(0, block_count - 1, cycle_turn, initial)
    pair, query_acc, key_gradient_total, total_value_gradient = visit_block(
        carry_state, block_count - 1
    )
    key_gradient_total, total_value_gradient = pass_grads(key_gradient_total, total_value_gradient)
    broad_zeros = jnp.zeros((rows_per_block, KEY_VALUE_HEADS * head_features), jnp.float32)
    key_broadcast = lax.dynamic_update_slice_in_dim(
        broad_zeros, key_gradient_total, kv_head * head_features, 1
    )
    value_wide = lax.dynamic_update_slice_in_dim(
        broad_zeros, total_value_gradient, kv_head * head_features, 1
    )
    key_part, value_part = scattered_sum(key_broadcast), scattered_sum(value_wide)
    keys_gradient = (logit_scale * key_part).astype(jnp.bfloat16)[None]
    values_gradient = value_part.astype(jnp.bfloat16)[None]
    query_out = (
        (logit_scale * query_acc)
        .astype(jnp.bfloat16)
        .reshape(1, rows_per_block, local_heads * head_features)
    )
    query_grad = lax.all_to_all(query_out, "head", split_axis=1, concat_axis=2, tiled=True)
    return (query_grad, keys_gradient, values_gradient)


def store_kernel(*refs):
    moves = [
        pltpu.make_async_copy(refs[i], refs[3 + i], refs[6].at[i]) for i in range(3)
    ]
    for move in moves:
        move.start()
    for move in moves:
        move.wait()


def store(*results):
    anywhere = pl.BlockSpec(memory_space=pl.ANY)
    return pl.pallas_call(
        store_kernel,
        out_shape=tuple(jax.ShapeDtypeStruct(x.shape, x.dtype) for x in results),
        in_specs=[anywhere] * 3,
        out_specs=(anywhere,) * 3,
        scratch_shapes=[pltpu.SemaphoreType.DMA((3,))],
    )(*results)


def shards(*arrays):
    lengths = arrays[-1]
    later = lax.broadcasted_iota(jnp.int32, lengths.shape, 0) > 0
    short = jnp.max(jnp.where(later, lengths, 0)) <= 1537
    return store(*lax.cond(short, fused, ring, *arrays))


def solution(mesh):
    in_specs = (
        P("blk", "head", None),
        P("blk", None, None),
        P("blk", None, None),
        P("blk", "head", None),
        P("blk", "head", None),
        P("blk", "head", None),
        P(),
    )
    out_specs = (P("blk", "head", None), P("blk", "head", None), P("blk", "head", None))
    return jax.shard_map(shards, mesh=mesh, in_specs=in_specs, out_specs=out_specs, check_vma=False)
```

```python
import functools

import jax
import jax.numpy as jnp
from jax import lax
from jax.experimental import pallas as pl
from jax.experimental.pallas import tpu as pltpu
from jax.sharding import PartitionSpec as P

QUERY_HEADS = 16
KEY_VALUE_HEADS = 2
BF = jnp.bfloat16
F32 = jnp.float32
SCALE = 128**-0.5
EXP2_SCALE = SCALE * 1.4426950408889634
FAR = 16384.0
MESH = pl.DeviceIdType.MESH


def split3(x):
    hi = x.astype(BF).astype(F32)
    rest = x - hi
    mid = rest.astype(BF).astype(F32)
    return hi, mid, rest - mid


def kernel(
    q_ref, k_ref, v_ref, o_ref, g_ref, lse_ref, len_ref,
    dq_ref, dk_ref, dv_ref,
    kvs, other, first_out, first_in, second_out, second_in, kept, last_out, last_in, direct_out, direct_in, held, mine,
    lse_all, here, swap, dq_out, dq_in,
    qn, gn, qta, gta, dqt, kt, dk, dv, aug,
    s_load, s_rows, s_own, r_own, s_x, r_x, s_spread, r_spread, s_relay, r_relay,
    s_first, r_first, s_second, r_second, s_last, r_last, s_direct, r_direct,
    s_lse, r_lse, s_swap, r_swap, s_dq, r_dq,
):
    y = lax.axis_index("head")
    b = lax.axis_index("blk")
    r = lax.rem(b, 2)
    sr = 1 - r
    c = b // 2
    row0 = b < 8
    rows = b >= 8
    cs = jnp.where(row0, c, c - 4)
    last = jnp.where(row0, 3, 27)
    prev1, next1 = cs >= 1, cs <= last - 1
    prev2, next2 = cs >= 2, cs <= last - 2
    first_chip = row0 & (cs == 0)
    last_chip = row0 & (cs == 3)
    second_chip = row0 & (cs == 1)
    sib = 2 * c + sr

    def copy(src, dst, send, recv, blk):
        return pltpu.make_async_remote_copy(
            src_ref=src, dst_ref=dst, send_sem=send, recv_sem=recv,
            device_id={"blk": blk}, device_id_type=MESH,
        )

    def head_cols(head, width):
        return pl.ds(pl.multiple_of(head * width, 128), width)

    loads = [
        pltpu.make_async_copy(ref.at[0, :, head_cols(head, 128)], dst.at[i], s_load.at[i, k])
        for k, (head, dst) in enumerate(((r, kvs.at[r]), (sr, other)))
        for i, ref in enumerate((k_ref, v_ref))
    ]
    row_loads = [
        pltpu.make_async_copy(ref.at[0, :, head_cols(r, 1024)], here.at[i], s_rows.at[i])
        for i, ref in enumerate((q_ref, g_ref, o_ref))
    ]
    for d in loads + row_loads:
        d.start()

    barrier = pltpu.get_barrier_semaphore()

    def greet(cond, blk):
        @pl.when(cond)
        def _():
            for core in range(2):
                pl.semaphore_signal(
                    barrier, inc=1, device_id={"blk": blk + core}, device_id_type=MESH
                )

        return jnp.where(cond, 2, 0)

    def greet_all(cond, blk):
        @pl.when(cond)
        def _():
            for i in range(8):
                pl.semaphore_signal(
                    barrier, inc=1, device_id=(i // 2, blk + i % 2), device_id_type=MESH
                )

        return jnp.where(cond, 8, 0)

    pl.semaphore_signal(barrier, inc=1, device_id={"blk": sib}, device_id_type=MESH)
    partners = 1 + greet(prev1, 2 * c - 2)
    partners += greet(next1, 2 * c + 2)
    partners += greet(prev2 & jnp.logical_not(last_chip), 2 * c - 4)
    partners += greet(next2 & jnp.logical_not(second_chip), 2 * c + 4)
    partners += greet_all(last_chip, 2 * c - 4)
    partners += greet_all(second_chip, 2 * c + 4)
    partners += greet(first_chip, 2 * c + 6)
    partners += greet(last_chip, 2 * c - 6)
    for i in range(1, 4):
        for core in range(2):
            pl.semaphore_signal(
                barrier, inc=1, device_id=(lax.rem(y + i, 4), 2 * c + core), device_id_type=MESH
            )
    pl.semaphore_wait(barrier, partners + 6)

    near_y = y + 1 - 2 * lax.rem(y, 2)
    ring_y = 3 - y
    over_y = lax.rem(y + 2, 4)

    def rows_of(q):
        return pl.ds(pl.multiple_of(q * 128, 128), 128)

    def to_chip(dist, slot, which):
        own, far, dst = kvs.at[r], other, kvs.at[slot]
        if dist == 2:
            own, far, dst = (x.at[:, rows_of(y)] for x in (own, far, dst))
        core = (r, sr)[which]
        return copy(
            (own, far)[which], dst, s_x.at[dist - 1, which], r_x.at[slot], 2 * (c + dist) + core
        )

    own_copy = copy(other, kvs.at[r], s_own, r_own, sib)

    def spread_copy(slot, a):
        part = kvs.at[slot, :, rows_of(y)]
        return pltpu.make_async_remote_copy(
            src_ref=part, dst_ref=part,
            send_sem=s_spread.at[slot, a], recv_sem=r_spread.at[slot, a],
            device_id=((near_y, ring_y)[a], b), device_id_type=MESH,
        )

    def spread_wait(slot, a):
        part = kvs.at[slot, :, rows_of((near_y, ring_y)[a])]
        pltpu.make_async_remote_copy(
            src_ref=part, dst_ref=part,
            send_sem=s_spread.at[slot, a], recv_sem=r_spread.at[slot, a],
            device_id=((near_y, ring_y)[a], b), device_id_type=MESH,
        ).wait_recv()

    def relay_copy(slot, a):
        part = kvs.at[slot, a, rows_of((ring_y, near_y)[a])]
        return pltpu.make_async_remote_copy(
            src_ref=part, dst_ref=part,
            send_sem=s_relay.at[slot, a], recv_sem=r_relay.at[slot, a],
            device_id=((near_y, ring_y)[a], b), device_id_type=MESH,
        )

    def relay_wait(slot, a):
        part = kvs.at[slot, a, rows_of(over_y)]
        pltpu.make_async_remote_copy(
            src_ref=part, dst_ref=part,
            send_sem=s_relay.at[slot, a], recv_sem=r_relay.at[slot, a],
            device_id=((near_y, ring_y)[a], b), device_id_type=MESH,
        ).wait_recv()

    def spread(slot):
        part = kvs.at[slot, :, rows_of(y)]
        copy(part, part, s_own, r_x.at[slot], sib).wait_recv()
        for a in range(2):
            spread_copy(slot, a).start()

    def relay(slot):
        for a in range(2):
            spread_wait(slot, 1 - a)
            relay_copy(slot, a).start()

    def swap_copy(i):
        src = (q_ref, g_ref, o_ref)[i]
        return copy(src.at[0, :, head_cols(sr, 1024)], swap.at[i], s_swap.at[i], r_swap.at[i], sib)

    stat_core = y // 2
    stat_here = r == stat_core

    def lse_tokens(peer):
        return lse_ref.at[0, :, pl.ds(pl.multiple_of(peer * 128, 128), 128)]

    def lse_copy(i):
        peer = lax.rem(y + i, 4)
        return pltpu.make_async_remote_copy(
            src_ref=lse_tokens(peer), dst_ref=lse_all.at[r, lax.rem(y, 2)],
            send_sem=s_lse.at[i], recv_sem=r_lse.at[r, lax.rem(y, 2)],
            device_id=(peer, 2 * c + stat_core), device_id_type=MESH,
        )

    sends_two = next2 & (row0 | (r == 1))

    def to_chips(act):
        def at(cond, dist, slot, which):
            @pl.when(cond)
            def _():
                act(to_chip(dist, slot, which))

        at(next1, 1, 2 + r, 0)
        at(first_chip, 3, 6 + r, 0)
        at(sends_two, 2, 4 + r, 0)
        at(sends_two, 2, 4 + r, 1)
        at(next1, 1, 2 + r, 1)
        at(first_chip, 3, 6 + r, 1)

    for i in range(3):
        swap_copy(i).start()
    for d in loads:
        d.wait()
    own_copy.start()
    to_chips(lambda d: d.start())
    for i in range(1, 4):
        lse_copy(i).start()

    @pl.when(stat_here)
    def _():
        mine_too = pltpu.make_async_copy(lse_tokens(y), lse_all.at[r, lax.rem(y, 2)], s_lse.at[0])
        mine_too.start()
        mine_too.wait()

    @pl.when(jnp.logical_not(stat_here))
    def _():
        lse_copy(0).start()

    lane = lax.broadcasted_iota(jnp.int32, (8, 128), 1)
    row = lax.broadcasted_iota(jnp.int32, (32, 128), 0)
    lo_l = jnp.zeros((8, 128), jnp.int32)
    len_l = jnp.zeros((8, 128), jnp.int32)
    lo_r = jnp.zeros((32, 128), jnp.int32)
    len_r = jnp.zeros((32, 128), jnp.int32)
    for i in range(32):
        n = len_ref[i]
        lo_l += jnp.where(lane > i, n, 0)
        len_l += jnp.where(lane == i, n, 0)
        lo_r += jnp.where(row > i, n, 0)
        len_r += jnp.where(row == i, n, 0)
    hi_l = lo_l + len_l
    aug_row = lax.broadcasted_iota(jnp.int32, (128, 128), 0)

    def prepare(block, q_of, g_of, o_of):
        for h in range(8):
            ch, o = block * 4 + h // 2, (h % 2) * 128
            qh, gh, oh = q_of(h), g_of(h), o_of(h)
            gt = gh.T
            qn[ch, o : o + 128, :] = qh
            gn[ch, o : o + 128, :] = gh
            qta[ch, 0:128, o : o + 128] = qh.T
            gta[ch, 0:128, o : o + 128] = gt
            delta = jnp.sum(gt.astype(F32) * oh.T.astype(F32), axis=0, keepdims=True)
            d0, d1, d2 = split3(-delta)
            extra = jnp.where(aug_row == 32, d0, 0.0)
            extra = jnp.where(aug_row == 33, d1, extra)
            extra = jnp.where(aug_row == 34, d2, extra)
            gta[ch, 128:256, o : o + 128] = extra.astype(BF)

    def prepare_stats(block):
        qpos = (2 * c + block) * 512 + y * 128 + lax.broadcasted_iota(jnp.int32, (32, 128), 1)
        doc_rows = jnp.where((qpos >= lo_r) & (qpos < lo_r + len_r), 0.0, -FAR)
        doc_rows = jnp.concatenate([doc_rows, jnp.zeros((96, 128), F32)], 0)
        for h in range(8):
            ch, o = block * 4 + h // 2, (h % 2) * 128
            stat = lse_all[block, h // 4, h % 4 : h % 4 + 1, :] * (-(128.0**0.5))
            d0, d1, d2 = split3(stat)
            extra = jnp.where(aug_row == 32, d0, doc_rows)
            extra = jnp.where(aug_row == 33, d1, extra)
            extra = jnp.where(aug_row == 34, d2, extra)
            qta[ch, 128:256, o : o + 128] = extra.astype(BF)

    def rows_in(ref):
        return [lambda h, i=i: ref[i, :, h * 128 : (h + 1) * 128] for i in range(3)]

    def lse_wait(block, half):
        @pl.when(jnp.logical_not((block == r) & (y == 2 * r + half)))
        def _():
            pltpu.make_async_remote_copy(
                src_ref=lse_all.at[block, half], dst_ref=lse_all.at[block, half],
                send_sem=s_lse.at[0], recv_sem=r_lse.at[block, half],
                device_id=(y, sib), device_id_type=MESH,
            ).wait_recv()

    dqt[...] = jnp.zeros_like(dqt)
    for d in row_loads:
        d.wait()
    prepare(r, *rows_in(here))
    for i in range(3):
        swap_copy(i).wait_recv()
    prepare(sr, *rows_in(swap))
    for block in range(2):
        for half in range(2):
            lse_wait(block, half)
        prepare_stats(block)

    def tile(slot):
        lane_k = lax.broadcasted_iota(jnp.int32, (512, 128), 1)
        kpos = (2 * (c - slot // 2) + lax.rem(slot, 2)) * 512
        kpos = kpos + lax.broadcasted_iota(jnp.int32, (512, 128), 0)
        inside = (kpos >= lo_l[0:1]) & (kpos < hi_l[0:1])
        ones = (lane_k >= 32) & (lane_k < 35)
        aug[...] = jnp.where(inside | ones, 1.0, 0.0).astype(BF)
        kt[...] = kvs[slot, 0].T
        whole = (slot >= 2) & jnp.logical_not(rows & (slot == 5))

        def scores(kj, vj, ch, causal):
            st = jnp.dot(kj, qta[ch], preferred_element_type=F32)
            p = jnp.exp2(st * EXP2_SCALE)
            if causal:
                krow = lax.broadcasted_iota(jnp.int32, (512, 256), 0)
                qcol = lax.broadcasted_iota(jnp.int32, (512, 256), 1) & 127
                p = jnp.where(krow <= qcol + y * 128, p, 0.0)
            dp = jnp.dot(vj, gta[ch], preferred_element_type=F32)
            return p.astype(BF), (p * dp).astype(BF)

        def gradients(pair, ch, first):
            dvi = jnp.dot(pair[0], gn[ch], preferred_element_type=F32)
            dki = jnp.dot(pair[1], qn[ch], preferred_element_type=F32)
            if first:
                dv[...] = dvi
                dk[...] = dki
            else:
                dv[...] += dvi
                dk[...] += dki
            dqt[ch] += jnp.dot(kt[...], pair[1], preferred_element_type=F32)

        def part(chunks, causal, first):
            kj = jnp.concatenate([kvs[slot, 0], aug[...]], 1)
            vj = jnp.concatenate([kvs[slot, 1], aug[...]], 1)
            pair = scores(kj, vj, chunks[0], causal)
            for i, ch in enumerate(chunks):
                later = scores(kj, vj, chunks[i + 1], causal) if i + 1 < len(chunks) else None
                gradients(pair, ch, first and i == 0)
                pair = later

        @pl.when(whole & jnp.logical_not(goes_direct(slot)))
        def _():
            part(range(8), False, True)

        @pl.when(goes_direct(slot))
        def _():
            kj = jnp.concatenate([kvs[slot, 0], aug[...]], 1)
            vj = jnp.concatenate([kvs[slot, 1], aug[...]], 1)

            def probs(ch):
                p = jnp.exp2(jnp.dot(kj, qta[ch], preferred_element_type=F32) * EXP2_SCALE)
                held[ch] = p
                return p.astype(BF)

            def dscores(ch):
                dp = jnp.dot(vj, gta[ch], preferred_element_type=F32)
                return (held[ch] * dp).astype(BF)

            now = probs(0)
            for ch in range(8):
                later = probs(ch + 1) if ch < 7 else None
                dvi = jnp.dot(now, gn[ch], preferred_element_type=F32)
                dv[...] = dvi if ch == 0 else dv[...] + dvi
                now = later
            direct(slot, 1)
            now = dscores(0)
            for ch in range(8):
                later = dscores(ch + 1) if ch < 7 else None
                dki = jnp.dot(now, qn[ch], preferred_element_type=F32)
                dk[...] = dki if ch == 0 else dk[...] + dki
                dqt[ch] += jnp.dot(kt[...], now, preferred_element_type=F32)
                now = later

        @pl.when(jnp.logical_not(whole))
        def _():
            dk[...] = jnp.zeros_like(dk)
            dv[...] = jnp.zeros_like(dv)

            @pl.when(slot < 2)
            def _():
                part([slot * 4 + i for i in range(4)], True, False)

            @pl.when(slot != 1)
            def _():
                block = jnp.where(slot == 0, 1, 0)
                part([block * 4 + i for i in range(4)], False, False)

    steps = 2 + jnp.where(row0, 2 * cs, jnp.where(cs >= 2, 3, 2 * cs))

    def slot_of(n):
        m = n - 2
        far = jnp.where(m < 4, 2 + 4 * lax.rem(m, 2) + lax.rem(r + m // 2, 2), 4 + lax.rem(r + m, 2))
        usual = 2 + 2 * (m // 2) + lax.rem(r + m, 2)
        usual = jnp.where(rows & (m == 2), 5, usual)
        return jnp.where(n < 2, n, jnp.where(last_chip, far, usual))

    def quarter(ref, q):
        return ref[rows_of(q), :]

    def first_copy(slot, a):
        return pltpu.make_async_remote_copy(
            src_ref=first_out.at[slot, a], dst_ref=first_in.at[slot, a],
            send_sem=s_first.at[slot, a], recv_sem=r_first.at[slot, a],
            device_id=((near_y, ring_y)[a], b), device_id_type=MESH,
        )

    def second_copy(slot, a):
        return pltpu.make_async_remote_copy(
            src_ref=second_out.at[slot, a], dst_ref=second_in.at[slot, a],
            send_sem=s_second.at[slot, a], recv_sem=r_second.at[slot, a],
            device_id=((ring_y, near_y)[a], b), device_id_type=MESH,
        )

    def last_copy(slot):
        dist = slot // 2
        return copy(
            last_out.at[slot], last_in.at[dist, r], s_last.at[slot], r_last.at[dist, r],
            2 * (c - dist) + lax.rem(slot, 2),
        )

    def first_exchange(slot):
        for a, total, one, two in ((0, dk, near_y, ring_y), (1, dv, ring_y, near_y)):
            first_out[slot, a, 0] = quarter(total, one).astype(BF)
            first_out[slot, a, 1] = quarter(total, over_y).astype(BF)
            first_copy(slot, a).start()
            kept[slot, a, 0] = quarter(total, y)
            kept[slot, a, 1] = quarter(total, two)

    def goes_direct(slot):
        return last_chip & (slot == 4 + sr)

    def direct_copy(slot, i, a):
        p, q = lax.rem(slot, 2), lax.rem(y + i, 4)
        return pltpu.make_async_remote_copy(
            src_ref=direct_out.at[p, i, a], dst_ref=direct_in.at[r, i, a],
            send_sem=s_direct.at[p, i, a], recv_sem=r_direct.at[r, i, a],
            device_id=(q, 2 * (c - 2) + p), device_id_type=MESH,
        )

    def direct(slot, a):
        p = lax.rem(slot, 2)
        for i in range(4):
            q = lax.rem(y + i, 4)
            direct_out[p, i, a] = quarter((dk, dv)[a], q).astype(BF)
            direct_copy(slot, i, a).start()

    def second_exchange(slot):
        for a in range(2):
            first_copy(slot, a).wait_recv()
            second_out[slot, a] = (kept[slot, a, 1] + first_in[slot, a, 1].astype(F32)).astype(BF)
            second_copy(slot, a).start()
            kept[slot, a, 0] += first_in[slot, a, 0].astype(F32)

    def hand_over(slot):
        for a in range(2):
            second_copy(slot, a).wait_recv()
            kept[slot, a, 0] += second_in[slot, a].astype(F32)

        @pl.when(slot == r)
        def _():
            for a in range(2):
                mine[a] = kept[slot, a, 0]

        @pl.when(slot != r)
        def _():
            for a in range(2):
                last_out[slot, a] = kept[slot, a, 0].astype(BF)
            last_copy(slot).start()

    dq_copy = copy(dq_out, dq_in, s_dq, r_dq, sib)

    def query_gradients():
        for h in range(8):
            o = (h % 2) * 128
            dq_out[:, h * 128 : (h + 1) * 128] = (
                (dqt[sr * 4 + h // 2, :, o : o + 128] * SCALE).T.astype(BF)
            )
        dq_copy.start()
        for h in range(8):
            o = (h % 2) * 128
            cols = pl.ds(pl.multiple_of(r * 1024 + h * 128, 128), 128)
            dq_ref[0, :, cols] = (dqt[r * 4 + h // 2, :, o : o + 128] * SCALE).T.astype(BF)

    copy(kvs.at[sr], kvs.at[sr], s_own, r_own, sib).wait_recv()

    def step(n, carry):
        @pl.when(n < steps)
        def _():
            slot = slot_of(n)

            @pl.when((n >= 2) & (slot // 2 == 2))
            def _():
                for a in range(2):
                    relay_wait(slot, a)

            @pl.when((n >= 2) & (slot // 2 != 2))
            def _():
                copy(kvs.at[slot], kvs.at[slot], s_own, r_x.at[slot], sib).wait_recv()

            tile(slot)

            @pl.when(goes_direct(slot))
            def _():
                direct(slot, 0)

            @pl.when(jnp.logical_not(goes_direct(slot)))
            def _():
                first_exchange(slot)

        @pl.when((n == jnp.where(last_chip, 2, 1)) & prev2)
        def _():
            spread(5)

            @pl.when(row0)
            def _():
                spread(4)

        @pl.when((n == jnp.where(last_chip, 4, 2)) & prev2)
        def _():
            relay(5)

            @pl.when(row0)
            def _():
                relay(4)

        @pl.when(n == steps)
        def _():
            query_gradients()

        @pl.when((n >= 2) & (n <= steps + 1))
        def _():
            slot = slot_of(n - 2)

            @pl.when(jnp.logical_not(goes_direct(slot)))
            def _():
                second_exchange(slot)

        @pl.when(n >= 4)
        def _():
            slot = slot_of(n - 4)

            @pl.when(jnp.logical_not(goes_direct(slot)))
            def _():
                hand_over(slot)

        return carry

    lax.fori_loop(0, steps + 4, step, 0)

    dq_copy.wait_recv()
    dq_ref[0, :, pl.ds(pl.multiple_of(sr * 1024, 1024), 1024)] = dq_in[...]

    def last_wait(dist, head):
        copy(
            last_in.at[dist, head], last_in.at[dist, head], s_last.at[0], r_last.at[dist, head], sib
        ).wait_recv()
        mine[...] += last_in[dist, head].astype(F32)

    def finish(head):
        @pl.when(next1)
        def _():
            last_wait(1, head)

        straight = second_chip & (head == sr)

        @pl.when(sends_two & jnp.logical_not(straight))
        def _():
            last_wait(2, head)

        @pl.when(straight)
        def _():
            for a in (1, 0):
                for i in range(4):
                    part = direct_in.at[head, i, a]
                    copy(part, part, s_own, r_direct.at[head, i, a], sib).wait_recv()
                    mine[a] += part[...].astype(F32)

        @pl.when(first_chip)
        def _():
            last_wait(3, head)

        cols = pl.ds(pl.multiple_of(head * 128, 128), 128)
        dk_ref[0, :, cols] = (mine[0] * SCALE).astype(BF)
        dv_ref[0, :, cols] = mine[1].astype(BF)

    finish(r)
    mine[...] = jnp.zeros_like(mine)
    last_wait(0, sr)
    finish(sr)

    for i in range(3):
        swap_copy(i).wait_send()
    own_copy.wait_send()
    dq_copy.wait_send()
    for i in range(1, 4):
        lse_copy(i).wait_send()

    @pl.when(jnp.logical_not(stat_here))
    def _():
        lse_copy(0).wait_send()

    def sent(n, carry):
        slot = slot_of(n)

        @pl.when(goes_direct(slot))
        def _():
            for i in range(4):
                for a in range(2):
                    direct_copy(slot, i, a).wait_send()

        @pl.when(jnp.logical_not(goes_direct(slot)))
        def _():
            for a in range(2):
                first_copy(slot, a).wait_send()
                second_copy(slot, a).wait_send()

        @pl.when((slot != r) & jnp.logical_not(goes_direct(slot)))
        def _():
            last_copy(slot).wait_send()

        @pl.when((n >= 2) & (slot // 2 == 2))
        def _():
            for a in range(2):
                spread_copy(slot, a).wait_send()
                relay_copy(slot, a).wait_send()

        return carry

    lax.fori_loop(0, steps, sent, 0)

    to_chips(lambda d: d.wait_send())


def fused(queries, keys, values, outputs, output_gradient, log_norms, doc_lengths):
    vmem = pl.BlockSpec(memory_space=pltpu.VMEM)
    dma = pltpu.SemaphoreType.DMA
    return pl.pallas_call(
        kernel,
        out_shape=(
            jax.ShapeDtypeStruct((1, 128, 2048), BF),
            jax.ShapeDtypeStruct((1, 128, 256), BF),
            jax.ShapeDtypeStruct((1, 128, 256), BF),
        ),
        in_specs=[pl.BlockSpec(memory_space=pl.ANY)] * 6 + [pl.BlockSpec(memory_space=pltpu.SMEM)],
        out_specs=(vmem, vmem, vmem),
        scratch_shapes=[
            pltpu.VMEM((8, 2, 512, 128), BF),
            pltpu.VMEM((2, 512, 128), BF),
            pltpu.VMEM((8, 2, 2, 128, 128), BF),
            pltpu.VMEM((8, 2, 2, 128, 128), BF),
            pltpu.VMEM((8, 2, 128, 128), BF),
            pltpu.VMEM((8, 2, 128, 128), BF),
            pltpu.VMEM((8, 2, 2, 128, 128), F32),
            pltpu.VMEM((8, 2, 128, 128), BF),
            pltpu.VMEM((4, 2, 2, 128, 128), BF),
            pltpu.VMEM((2, 4, 2, 128, 128), BF),
            pltpu.VMEM((2, 4, 2, 128, 128), BF),
            pltpu.VMEM((8, 512, 256), F32),
            pltpu.VMEM((2, 128, 128), F32),
            pltpu.VMEM((2, 2, 4, 128), F32),
            pltpu.VMEM((3, 128, 1024), BF),
            pltpu.VMEM((3, 128, 1024), BF),
            pltpu.VMEM((128, 1024), BF),
            pltpu.VMEM((128, 1024), BF),
            pltpu.VMEM((8, 256, 128), BF),
            pltpu.VMEM((8, 256, 128), BF),
            pltpu.VMEM((8, 256, 256), BF),
            pltpu.VMEM((8, 256, 256), BF),
            pltpu.VMEM((8, 128, 256), F32),
            pltpu.VMEM((128, 512), BF),
            pltpu.VMEM((512, 128), F32),
            pltpu.VMEM((512, 128), F32),
            pltpu.VMEM((512, 128), BF),
            dma((2, 2)), dma((3,)), dma, dma, dma((3, 2)), dma((8,)), dma((8, 2)), dma((8, 2)), dma((8, 2)), dma((8, 2)),
            dma((8, 2)), dma((8, 2)), dma((8, 2)), dma((8, 2)), dma((8,)), dma((4, 2)), dma((2, 4, 2)), dma((2, 4, 2)),
            dma((4,)), dma((2, 2)), dma((3,)), dma((3,)), dma, dma,
        ],
        compiler_params=pltpu.CompilerParams(
            collective_id=0, has_side_effects=True, vmem_limit_bytes=56 * 2**20
        ),
    )(queries, keys, values, outputs, output_gradient, log_norms, doc_lengths)


def passed_along(x, axis, by):
    peers = lax.axis_size(axis)
    return lax.ppermute(x, axis, [(i, (i + by) % peers) for i in range(peers)])


def shifted(block, axis, distance):
    devices = range(lax.axis_size(axis))
    route = [(i - distance, i) for i in devices if i - distance in devices]
    return lax.ppermute(block, axis, route)


def doc_starts(doc_lengths, positions):
    firsts = jnp.cumsum(doc_lengths) - doc_lengths
    return jnp.max(jnp.where(firsts[None, :] <= positions[:, None], firsts[None, :], 0), axis=1)


def pass_grads(key_gradient_total, total_value_gradient):
    return passed_along((key_gradient_total, total_value_gradient), "blk", 1)


def scattered_sum(x):
    parts = x.reshape(4, x.shape[0] // 4, x.shape[1])
    return jnp.sum(lax.all_to_all(parts, "head", split_axis=0, concat_axis=0), axis=0)


def ring(queries, keys, values, outputs, output_gradient, log_norms, doc_lengths):
    block_count = lax.axis_size("blk")
    block_index = lax.axis_index("blk")
    every_query, every_output, grad_all = (
        lax.all_to_all(queries, "head", split_axis=2, concat_axis=1, tiled=True),
        lax.all_to_all(outputs, "head", split_axis=2, concat_axis=1, tiled=True),
        lax.all_to_all(output_gradient, "head", split_axis=2, concat_axis=1, tiled=True),
    )
    rows_per_block = every_query.shape[1]
    head_features = keys.shape[2] // KEY_VALUE_HEADS
    local_heads = every_query.shape[2] // head_features
    query_group_size = QUERY_HEADS // KEY_VALUE_HEADS
    logit_scale = head_features ** (-0.5)
    query_loc = every_query[0].reshape(rows_per_block, local_heads, head_features)
    grad_loc = grad_all[0].reshape(rows_per_block, local_heads, head_features)
    output_loc = every_output[0].reshape(rows_per_block, local_heads, head_features)
    row_delta = jnp.sum(grad_loc.astype(jnp.float32) * output_loc.astype(jnp.float32), axis=-1).T
    row_statistics = log_norms[0]
    kv_head = lax.axis_index("head") * local_heads // query_group_size
    key_own = lax.dynamic_slice_in_dim(keys[0], kv_head * head_features, head_features, 1)
    value_own = lax.dynamic_slice_in_dim(values[0], kv_head * head_features, head_features, 1)
    query_pos = block_index * rows_per_block + jnp.arange(rows_per_block, dtype=jnp.int32)
    first_pos = doc_starts(doc_lengths, query_pos)

    def tile_grads(pair, key_block):
        key_blk, value_blk = pair
        key_pos = key_block * rows_per_block + jnp.arange(rows_per_block, dtype=jnp.int32)
        allowed = (key_pos[None, :] <= query_pos[:, None]) & (
            key_pos[None, :] >= first_pos[:, None]
        )
        scores = logit_scale * jnp.einsum(
            "qhd,kd->hqk", query_loc, key_blk, preferred_element_type=jnp.float32
        )
        probability = jnp.where(allowed[None], jnp.exp(scores - row_statistics[:, :, None]), 0.0)
        prob_low = probability.astype(jnp.bfloat16)
        value_add = jnp.einsum(
            "hqk,qhd->kd", prob_low, grad_loc, preferred_element_type=jnp.float32
        )
        dprob = jnp.einsum("qhd,kd->hqk", grad_loc, value_blk, preferred_element_type=jnp.float32)
        dscore = (probability * (dprob - row_delta[:, :, None])).astype(jnp.bfloat16)
        query_add = jnp.einsum("hqk,kd->qhd", dscore, key_blk, preferred_element_type=jnp.float32)
        key_increment = jnp.einsum(
            "hqk,qhd->kd", dscore, query_loc, preferred_element_type=jnp.float32
        )
        return (query_add, key_increment, value_add)

    def no_grads():
        flat = jnp.zeros((rows_per_block, head_features), jnp.float32)
        return (jnp.zeros((rows_per_block, local_heads, head_features), jnp.float32), flat, flat)

    def visit_block(carry_state, cycle_step):
        pair, query_acc, key_gradient_total, total_value_gradient = carry_state
        key_block = (block_index - cycle_step) % block_count
        active = (key_block <= block_index) & ((key_block + 1) * rows_per_block - 1 >= first_pos[0])
        query_add, key_increment, value_add = lax.cond(
            active, lambda: tile_grads(pair, key_block), no_grads
        )
        return (
            pair,
            query_acc + query_add,
            key_gradient_total + key_increment,
            total_value_gradient + value_add,
        )

    def cycle_turn(cycle_step, carry_state):
        pair, query_acc, key_gradient_total, total_value_gradient = visit_block(
            carry_state, cycle_step
        )
        pair = shifted((pair[0], pair[1]), "blk", 1)
        key_gradient_total, total_value_gradient = pass_grads(
            key_gradient_total, total_value_gradient
        )
        return (pair, query_acc, key_gradient_total, total_value_gradient)

    flat_zero = jnp.zeros((rows_per_block, head_features), jnp.float32)
    initial = (
        (key_own, value_own),
        jnp.zeros((rows_per_block, local_heads, head_features), jnp.float32),
        flat_zero,
        flat_zero,
    )
    carry_state = lax.fori_loop(0, block_count - 1, cycle_turn, initial)
    pair, query_acc, key_gradient_total, total_value_gradient = visit_block(
        carry_state, block_count - 1
    )
    key_gradient_total, total_value_gradient = pass_grads(key_gradient_total, total_value_gradient)
    broad_zeros = jnp.zeros((rows_per_block, KEY_VALUE_HEADS * head_features), jnp.float32)
    key_broadcast = lax.dynamic_update_slice_in_dim(
        broad_zeros, key_gradient_total, kv_head * head_features, 1
    )
    value_wide = lax.dynamic_update_slice_in_dim(
        broad_zeros, total_value_gradient, kv_head * head_features, 1
    )
    key_part, value_part = scattered_sum(key_broadcast), scattered_sum(value_wide)
    keys_gradient = (logit_scale * key_part).astype(jnp.bfloat16)[None]
    values_gradient = value_part.astype(jnp.bfloat16)[None]
    query_out = (
        (logit_scale * query_acc)
        .astype(jnp.bfloat16)
        .reshape(1, rows_per_block, local_heads * head_features)
    )
    query_grad = lax.all_to_all(query_out, "head", split_axis=1, concat_axis=2, tiled=True)
    return (query_grad, keys_gradient, values_gradient)


def store_kernel(*refs):
    moves = [
        pltpu.make_async_copy(refs[i], refs[3 + i], refs[6].at[i]) for i in range(3)
    ]
    for move in moves:
        move.start()
    for move in moves:
        move.wait()


def store(*results):
    anywhere = pl.BlockSpec(memory_space=pl.ANY)
    return pl.pallas_call(
        store_kernel,
        out_shape=tuple(jax.ShapeDtypeStruct(x.shape, x.dtype) for x in results),
        in_specs=[anywhere] * 3,
        out_specs=(anywhere,) * 3,
        scratch_shapes=[pltpu.SemaphoreType.DMA((3,))],
    )(*results)


def shards(*arrays):
    lengths = arrays[-1]
    later = lax.broadcasted_iota(jnp.int32, lengths.shape, 0) > 0
    short = jnp.max(jnp.where(later, lengths, 0)) <= 1537
    return store(*lax.cond(short, fused, ring, *arrays))


def solution(mesh):
    in_specs = (
        P("blk", "head", None),
        P("blk", None, None),
        P("blk", None, None),
        P("blk", "head", None),
        P("blk", "head", None),
        P("blk", "head", None),
        P(),
    )
    out_specs = (P("blk", "head", None), P("blk", "head", None), P("blk", "head", None))
    return jax.shard_map(shards, mesh=mesh, in_specs=in_specs, out_specs=out_specs, check_vma=False)
```

```python
import functools

import jax
import jax.numpy as jnp
from jax import lax
from jax.experimental import pallas as pl
from jax.experimental.pallas import tpu as pltpu
from jax.sharding import PartitionSpec as P

QUERY_HEADS = 16
KEY_VALUE_HEADS = 2
BF = jnp.bfloat16
F32 = jnp.float32
SCALE = 128**-0.5
EXP2_SCALE = SCALE * 1.4426950408889634
FAR = 16384.0
MESH = pl.DeviceIdType.MESH


def split3(x):
    hi = x.astype(BF).astype(F32)
    rest = x - hi
    mid = rest.astype(BF).astype(F32)
    return hi, mid, rest - mid


def kernel(
    q_ref, k_ref, v_ref, o_ref, g_ref, lse_ref, len_ref,
    dq_ref, dk_ref, dv_ref,
    kvs, other, first_out, first_in, second_out, second_in, kept, last_out, last_in, direct_out, direct_in, mine,
    lse_all, here, swap, dq_out, dq_in,
    qn, gn, qta, gta, dqt, kt, dk, dv, aug,
    s_load, s_rows, s_own, r_own, s_x, r_x, s_spread, r_spread, s_relay, r_relay,
    s_first, r_first, s_second, r_second, s_last, r_last, s_direct, r_direct,
    s_lse, r_lse, s_swap, r_swap, s_dq, r_dq,
):
    y = lax.axis_index("head")
    b = lax.axis_index("blk")
    r = lax.rem(b, 2)
    sr = 1 - r
    c = b // 2
    row0 = b < 8
    rows = b >= 8
    cs = jnp.where(row0, c, c - 4)
    last = jnp.where(row0, 3, 27)
    prev1, next1 = cs >= 1, cs <= last - 1
    prev2, next2 = cs >= 2, cs <= last - 2
    first_chip = row0 & (cs == 0)
    last_chip = row0 & (cs == 3)
    second_chip = row0 & (cs == 1)
    sib = 2 * c + sr

    def copy(src, dst, send, recv, blk):
        return pltpu.make_async_remote_copy(
            src_ref=src, dst_ref=dst, send_sem=send, recv_sem=recv,
            device_id={"blk": blk}, device_id_type=MESH,
        )

    def head_cols(head, width):
        return pl.ds(pl.multiple_of(head * width, 128), width)

    loads = [
        pltpu.make_async_copy(ref.at[0, :, head_cols(head, 128)], dst.at[i], s_load.at[i, k])
        for k, (head, dst) in enumerate(((r, kvs.at[r]), (sr, other)))
        for i, ref in enumerate((k_ref, v_ref))
    ]
    row_loads = [
        pltpu.make_async_copy(ref.at[0, :, head_cols(r, 1024)], here.at[i], s_rows.at[i])
        for i, ref in enumerate((q_ref, g_ref, o_ref))
    ]
    for d in loads + row_loads:
        d.start()

    barrier = pltpu.get_barrier_semaphore()

    def greet(cond, blk):
        @pl.when(cond)
        def _():
            for core in range(2):
                pl.semaphore_signal(
                    barrier, inc=1, device_id={"blk": blk + core}, device_id_type=MESH
                )

        return jnp.where(cond, 2, 0)

    def greet_all(cond, blk):
        @pl.when(cond)
        def _():
            for i in range(8):
                pl.semaphore_signal(
                    barrier, inc=1, device_id=(i // 2, blk + i % 2), device_id_type=MESH
                )

        return jnp.where(cond, 8, 0)

    pl.semaphore_signal(barrier, inc=1, device_id={"blk": sib}, device_id_type=MESH)
    partners = 1 + greet(prev1, 2 * c - 2)
    partners += greet(next1, 2 * c + 2)
    partners += greet(prev2 & jnp.logical_not(last_chip), 2 * c - 4)
    partners += greet(next2 & jnp.logical_not(second_chip), 2 * c + 4)
    partners += greet_all(last_chip, 2 * c - 4)
    partners += greet_all(second_chip, 2 * c + 4)
    partners += greet(first_chip, 2 * c + 6)
    partners += greet(last_chip, 2 * c - 6)
    for i in range(1, 4):
        for core in range(2):
            pl.semaphore_signal(
                barrier, inc=1, device_id=(lax.rem(y + i, 4), 2 * c + core), device_id_type=MESH
            )
    pl.semaphore_wait(barrier, partners + 6)

    near_y = y + 1 - 2 * lax.rem(y, 2)
    ring_y = 3 - y
    over_y = lax.rem(y + 2, 4)

    def rows_of(q):
        return pl.ds(pl.multiple_of(q * 128, 128), 128)

    def to_chip(dist, slot, which):
        own, far, dst = kvs.at[r], other, kvs.at[slot]
        if dist == 2:
            own, far, dst = (x.at[:, rows_of(y)] for x in (own, far, dst))
        core = (r, sr)[which]
        return copy(
            (own, far)[which], dst, s_x.at[dist - 1, which], r_x.at[slot], 2 * (c + dist) + core
        )

    own_copy = copy(other, kvs.at[r], s_own, r_own, sib)

    def spread_copy(slot, a):
        part = kvs.at[slot, :, rows_of(y)]
        return pltpu.make_async_remote_copy(
            src_ref=part, dst_ref=part,
            send_sem=s_spread.at[slot, a], recv_sem=r_spread.at[slot, a],
            device_id=((near_y, ring_y)[a], b), device_id_type=MESH,
        )

    def spread_wait(slot, a):
        part = kvs.at[slot, :, rows_of((near_y, ring_y)[a])]
        pltpu.make_async_remote_copy(
            src_ref=part, dst_ref=part,
            send_sem=s_spread.at[slot, a], recv_sem=r_spread.at[slot, a],
            device_id=((near_y, ring_y)[a], b), device_id_type=MESH,
        ).wait_recv()

    def relay_copy(slot, a):
        part = kvs.at[slot, a, rows_of((ring_y, near_y)[a])]
        return pltpu.make_async_remote_copy(
            src_ref=part, dst_ref=part,
            send_sem=s_relay.at[slot, a], recv_sem=r_relay.at[slot, a],
            device_id=((near_y, ring_y)[a], b), device_id_type=MESH,
        )

    def relay_wait(slot, a):
        part = kvs.at[slot, a, rows_of(over_y)]
        pltpu.make_async_remote_copy(
            src_ref=part, dst_ref=part,
            send_sem=s_relay.at[slot, a], recv_sem=r_relay.at[slot, a],
            device_id=((near_y, ring_y)[a], b), device_id_type=MESH,
        ).wait_recv()

    def spread(slot):
        part = kvs.at[slot, :, rows_of(y)]
        copy(part, part, s_own, r_x.at[slot], sib).wait_recv()
        for a in range(2):
            spread_copy(slot, a).start()

    def relay(slot):
        for a in range(2):
            spread_wait(slot, 1 - a)
            relay_copy(slot, a).start()

    def swap_copy(i):
        src = (q_ref, g_ref, o_ref)[i]
        return copy(src.at[0, :, head_cols(sr, 1024)], swap.at[i], s_swap.at[i], r_swap.at[i], sib)

    stat_core = y // 2
    stat_here = r == stat_core

    def lse_tokens(peer):
        return lse_ref.at[0, :, pl.ds(pl.multiple_of(peer * 128, 128), 128)]

    def lse_copy(i):
        peer = lax.rem(y + i, 4)
        return pltpu.make_async_remote_copy(
            src_ref=lse_tokens(peer), dst_ref=lse_all.at[r, lax.rem(y, 2)],
            send_sem=s_lse.at[i], recv_sem=r_lse.at[r, lax.rem(y, 2)],
            device_id=(peer, 2 * c + stat_core), device_id_type=MESH,
        )

    sends_two = next2 & (row0 | (r == 1))

    def to_chips(act):
        def at(cond, dist, slot, which):
            @pl.when(cond)
            def _():
                act(to_chip(dist, slot, which))

        at(next1, 1, 2 + r, 0)
        at(first_chip, 3, 6 + r, 0)
        at(sends_two, 2, 4 + r, 0)
        at(sends_two, 2, 4 + r, 1)
        at(next1, 1, 2 + r, 1)
        at(first_chip, 3, 6 + r, 1)

    for i in range(3):
        swap_copy(i).start()
    for d in loads:
        d.wait()
    own_copy.start()
    to_chips(lambda d: d.start())
    for i in range(1, 4):
        lse_copy(i).start()

    @pl.when(stat_here)
    def _():
        mine_too = pltpu.make_async_copy(lse_tokens(y), lse_all.at[r, lax.rem(y, 2)], s_lse.at[0])
        mine_too.start()
        mine_too.wait()

    @pl.when(jnp.logical_not(stat_here))
    def _():
        lse_copy(0).start()

    lane = lax.broadcasted_iota(jnp.int32, (8, 128), 1)
    row = lax.broadcasted_iota(jnp.int32, (32, 128), 0)
    lo_l = jnp.zeros((8, 128), jnp.int32)
    len_l = jnp.zeros((8, 128), jnp.int32)
    lo_r = jnp.zeros((32, 128), jnp.int32)
    len_r = jnp.zeros((32, 128), jnp.int32)
    for i in range(32):
        n = len_ref[i]
        lo_l += jnp.where(lane > i, n, 0)
        len_l += jnp.where(lane == i, n, 0)
        lo_r += jnp.where(row > i, n, 0)
        len_r += jnp.where(row == i, n, 0)
    hi_l = lo_l + len_l
    aug_row = lax.broadcasted_iota(jnp.int32, (128, 128), 0)

    def prepare(block, q_of, g_of, o_of):
        for h in range(8):
            ch, o = block * 4 + h // 2, (h % 2) * 128
            qh, gh, oh = q_of(h), g_of(h), o_of(h)
            gt = gh.T
            qn[ch, o : o + 128, :] = qh
            gn[ch, o : o + 128, :] = gh
            qta[ch, 0:128, o : o + 128] = qh.T
            gta[ch, 0:128, o : o + 128] = gt
            delta = jnp.sum(gt.astype(F32) * oh.T.astype(F32), axis=0, keepdims=True)
            d0, d1, d2 = split3(-delta)
            extra = jnp.where(aug_row == 32, d0, 0.0)
            extra = jnp.where(aug_row == 33, d1, extra)
            extra = jnp.where(aug_row == 34, d2, extra)
            gta[ch, 128:256, o : o + 128] = extra.astype(BF)

    def prepare_stats(block):
        qpos = (2 * c + block) * 512 + y * 128 + lax.broadcasted_iota(jnp.int32, (32, 128), 1)
        doc_rows = jnp.where((qpos >= lo_r) & (qpos < lo_r + len_r), 0.0, -FAR)
        doc_rows = jnp.concatenate([doc_rows, jnp.zeros((96, 128), F32)], 0)
        for h in range(8):
            ch, o = block * 4 + h // 2, (h % 2) * 128
            stat = lse_all[block, h // 4, h % 4 : h % 4 + 1, :] * (-(128.0**0.5))
            d0, d1, d2 = split3(stat)
            extra = jnp.where(aug_row == 32, d0, doc_rows)
            extra = jnp.where(aug_row == 33, d1, extra)
            extra = jnp.where(aug_row == 34, d2, extra)
            qta[ch, 128:256, o : o + 128] = extra.astype(BF)

    def rows_in(ref):
        return [lambda h, i=i: ref[i, :, h * 128 : (h + 1) * 128] for i in range(3)]

    def lse_wait(block, half):
        @pl.when(jnp.logical_not((block == r) & (y == 2 * r + half)))
        def _():
            pltpu.make_async_remote_copy(
                src_ref=lse_all.at[block, half], dst_ref=lse_all.at[block, half],
                send_sem=s_lse.at[0], recv_sem=r_lse.at[block, half],
                device_id=(y, sib), device_id_type=MESH,
            ).wait_recv()

    dqt[...] = jnp.zeros_like(dqt)
    for d in row_loads:
        d.wait()
    prepare(r, *rows_in(here))
    for i in range(3):
        swap_copy(i).wait_recv()
    prepare(sr, *rows_in(swap))
    for block in range(2):
        for half in range(2):
            lse_wait(block, half)
        prepare_stats(block)

    def tile(slot):
        lane_k = lax.broadcasted_iota(jnp.int32, (512, 128), 1)
        kpos = (2 * (c - slot // 2) + lax.rem(slot, 2)) * 512
        kpos = kpos + lax.broadcasted_iota(jnp.int32, (512, 128), 0)
        inside = (kpos >= lo_l[0:1]) & (kpos < hi_l[0:1])
        ones = (lane_k >= 32) & (lane_k < 35)
        aug[...] = jnp.where(inside | ones, 1.0, 0.0).astype(BF)
        kt[...] = kvs[slot, 0].T
        whole = (slot >= 2) & jnp.logical_not(rows & (slot == 5))

        def scores(kj, vj, ch, causal):
            st = jnp.dot(kj, qta[ch], preferred_element_type=F32)
            p = jnp.exp2(st * EXP2_SCALE)
            if causal:
                krow = lax.broadcasted_iota(jnp.int32, (512, 256), 0)
                qcol = lax.broadcasted_iota(jnp.int32, (512, 256), 1) & 127
                p = jnp.where(krow <= qcol + y * 128, p, 0.0)
            dp = jnp.dot(vj, gta[ch], preferred_element_type=F32)
            return p.astype(BF), (p * dp).astype(BF)

        def gradients(pair, ch, first):
            dvi = jnp.dot(pair[0], gn[ch], preferred_element_type=F32)
            dki = jnp.dot(pair[1], qn[ch], preferred_element_type=F32)
            if first:
                dv[...] = dvi
                dk[...] = dki
            else:
                dv[...] += dvi
                dk[...] += dki
            dqt[ch] += jnp.dot(kt[...], pair[1], preferred_element_type=F32)

        def part(chunks, causal, first):
            kj = jnp.concatenate([kvs[slot, 0], aug[...]], 1)
            vj = jnp.concatenate([kvs[slot, 1], aug[...]], 1)
            pair = scores(kj, vj, chunks[0], causal)
            for i, ch in enumerate(chunks):
                later = scores(kj, vj, chunks[i + 1], causal) if i + 1 < len(chunks) else None
                gradients(pair, ch, first and i == 0)
                pair = later

        @pl.when(whole)
        def _():
            part(range(8), False, True)

        @pl.when(jnp.logical_not(whole))
        def _():
            dk[...] = jnp.zeros_like(dk)
            dv[...] = jnp.zeros_like(dv)

            @pl.when(slot < 2)
            def _():
                part([slot * 4 + i for i in range(4)], True, False)

            @pl.when(slot != 1)
            def _():
                block = jnp.where(slot == 0, 1, 0)
                part([block * 4 + i for i in range(4)], False, False)

    steps = 2 + jnp.where(row0, 2 * cs, jnp.where(cs >= 2, 3, 2 * cs))

    def slot_of(n):
        m = n - 2
        far = jnp.where(m < 4, 2 + 4 * lax.rem(m, 2) + lax.rem(r + m // 2, 2), 4 + lax.rem(r + m, 2))
        usual = 2 + 2 * (m // 2) + lax.rem(r + m, 2)
        usual = jnp.where(rows & (m == 2), 5, usual)
        return jnp.where(n < 2, n, jnp.where(last_chip, far, usual))

    def quarter(ref, q):
        return ref[rows_of(q), :]

    def first_copy(slot, a):
        return pltpu.make_async_remote_copy(
            src_ref=first_out.at[slot, a], dst_ref=first_in.at[slot, a],
            send_sem=s_first.at[slot, a], recv_sem=r_first.at[slot, a],
            device_id=((near_y, ring_y)[a], b), device_id_type=MESH,
        )

    def second_copy(slot, a):
        return pltpu.make_async_remote_copy(
            src_ref=second_out.at[slot, a], dst_ref=second_in.at[slot, a],
            send_sem=s_second.at[slot, a], recv_sem=r_second.at[slot, a],
            device_id=((ring_y, near_y)[a], b), device_id_type=MESH,
        )

    def last_copy(slot):
        dist = slot // 2
        return copy(
            last_out.at[slot], last_in.at[dist, r], s_last.at[slot], r_last.at[dist, r],
            2 * (c - dist) + lax.rem(slot, 2),
        )

    def first_exchange(slot):
        for a, total, one, two in ((0, dk, near_y, ring_y), (1, dv, ring_y, near_y)):
            first_out[slot, a, 0] = quarter(total, one).astype(BF)
            first_out[slot, a, 1] = quarter(total, over_y).astype(BF)
            first_copy(slot, a).start()
            kept[slot, a, 0] = quarter(total, y)
            kept[slot, a, 1] = quarter(total, two)

    def goes_direct(slot):
        return last_chip & (slot == 4 + sr)

    def direct_copy(slot, i):
        p, q = lax.rem(slot, 2), lax.rem(y + i, 4)
        return pltpu.make_async_remote_copy(
            src_ref=direct_out.at[p, i], dst_ref=direct_in.at[r, i],
            send_sem=s_direct.at[p, i], recv_sem=r_direct.at[r, i],
            device_id=(q, 2 * (c - 2) + p), device_id_type=MESH,
        )

    def direct(slot):
        p = lax.rem(slot, 2)
        for i in range(4):
            q = lax.rem(y + i, 4)
            direct_out[p, i, 0] = quarter(dk, q).astype(BF)
            direct_out[p, i, 1] = quarter(dv, q).astype(BF)
            direct_copy(slot, i).start()

    def second_exchange(slot):
        for a in range(2):
            first_copy(slot, a).wait_recv()
            second_out[slot, a] = (kept[slot, a, 1] + first_in[slot, a, 1].astype(F32)).astype(BF)
            second_copy(slot, a).start()
            kept[slot, a, 0] += first_in[slot, a, 0].astype(F32)

    def hand_over(slot):
        for a in range(2):
            second_copy(slot, a).wait_recv()
            kept[slot, a, 0] += second_in[slot, a].astype(F32)

        @pl.when(slot == r)
        def _():
            for a in range(2):
                mine[a] = kept[slot, a, 0]

        @pl.when(slot != r)
        def _():
            for a in range(2):
                last_out[slot, a] = kept[slot, a, 0].astype(BF)
            last_copy(slot).start()

    dq_copy = copy(dq_out, dq_in, s_dq, r_dq, sib)

    def query_gradients():
        for h in range(8):
            o = (h % 2) * 128
            dq_out[:, h * 128 : (h + 1) * 128] = (
                (dqt[sr * 4 + h // 2, :, o : o + 128] * SCALE).T.astype(BF)
            )
        dq_copy.start()
        for h in range(8):
            o = (h % 2) * 128
            cols = pl.ds(pl.multiple_of(r * 1024 + h * 128, 128), 128)
            dq_ref[0, :, cols] = (dqt[r * 4 + h // 2, :, o : o + 128] * SCALE).T.astype(BF)

    copy(kvs.at[sr], kvs.at[sr], s_own, r_own, sib).wait_recv()

    def step(n, carry):
        @pl.when(n < steps)
        def _():
            slot = slot_of(n)

            @pl.when((n >= 2) & (slot // 2 == 2))
            def _():
                for a in range(2):
                    relay_wait(slot, a)

            @pl.when((n >= 2) & (slot // 2 != 2))
            def _():
                copy(kvs.at[slot], kvs.at[slot], s_own, r_x.at[slot], sib).wait_recv()

            tile(slot)

            @pl.when(goes_direct(slot))
            def _():
                direct(slot)

            @pl.when(jnp.logical_not(goes_direct(slot)))
            def _():
                first_exchange(slot)

        @pl.when((n == jnp.where(last_chip, 2, 1)) & prev2)
        def _():
            spread(5)

            @pl.when(row0)
            def _():
                spread(4)

        @pl.when((n == jnp.where(last_chip, 4, 2)) & prev2)
        def _():
            relay(5)

            @pl.when(row0)
            def _():
                relay(4)

        @pl.when(n == steps)
        def _():
            query_gradients()

        @pl.when((n >= 2) & (n <= steps + 1) & jnp.logical_not(last_chip & (n >= 6)))
        def _():
            slot = slot_of(n - 2)

            @pl.when(jnp.logical_not(goes_direct(slot)))
            def _():
                second_exchange(slot)

        @pl.when(last_chip & (n >= 5) & (n <= steps))
        def _():
            slot = slot_of(n - 1)

            @pl.when(jnp.logical_not(goes_direct(slot)))
            def _():
                second_exchange(slot)

        @pl.when(n >= 4)
        def _():
            slot = slot_of(n - 4)

            @pl.when(jnp.logical_not(goes_direct(slot)))
            def _():
                hand_over(slot)

        return carry

    lax.fori_loop(0, steps + 4, step, 0)

    dq_copy.wait_recv()
    dq_ref[0, :, pl.ds(pl.multiple_of(sr * 1024, 1024), 1024)] = dq_in[...]

    def last_wait(dist, head):
        copy(
            last_in.at[dist, head], last_in.at[dist, head], s_last.at[0], r_last.at[dist, head], sib
        ).wait_recv()
        mine[...] += last_in[dist, head].astype(F32)

    def finish(head):
        @pl.when(next1)
        def _():
            last_wait(1, head)

        straight = second_chip & (head == sr)

        @pl.when(sends_two & jnp.logical_not(straight))
        def _():
            last_wait(2, head)

        @pl.when(straight)
        def _():
            for i in range(4):
                copy(
                    direct_in.at[head, i], direct_in.at[head, i], s_own, r_direct.at[head, i], sib
                ).wait_recv()
                mine[...] += direct_in[head, i].astype(F32)

        @pl.when(first_chip)
        def _():
            last_wait(3, head)

        cols = pl.ds(pl.multiple_of(head * 128, 128), 128)
        dk_ref[0, :, cols] = (mine[0] * SCALE).astype(BF)
        dv_ref[0, :, cols] = mine[1].astype(BF)

    finish(r)
    mine[...] = jnp.zeros_like(mine)
    last_wait(0, sr)
    finish(sr)

    for i in range(3):
        swap_copy(i).wait_send()
    own_copy.wait_send()
    dq_copy.wait_send()
    for i in range(1, 4):
        lse_copy(i).wait_send()

    @pl.when(jnp.logical_not(stat_here))
    def _():
        lse_copy(0).wait_send()

    def sent(n, carry):
        slot = slot_of(n)

        @pl.when(goes_direct(slot))
        def _():
            for i in range(4):
                direct_copy(slot, i).wait_send()

        @pl.when(jnp.logical_not(goes_direct(slot)))
        def _():
            for a in range(2):
                first_copy(slot, a).wait_send()
                second_copy(slot, a).wait_send()

        @pl.when((slot != r) & jnp.logical_not(goes_direct(slot)))
        def _():
            last_copy(slot).wait_send()

        @pl.when((n >= 2) & (slot // 2 == 2))
        def _():
            for a in range(2):
                spread_copy(slot, a).wait_send()
                relay_copy(slot, a).wait_send()

        return carry

    lax.fori_loop(0, steps, sent, 0)

    to_chips(lambda d: d.wait_send())


def fused(queries, keys, values, outputs, output_gradient, log_norms, doc_lengths):
    vmem = pl.BlockSpec(memory_space=pltpu.VMEM)
    dma = pltpu.SemaphoreType.DMA
    return pl.pallas_call(
        kernel,
        out_shape=(
            jax.ShapeDtypeStruct((1, 128, 2048), BF),
            jax.ShapeDtypeStruct((1, 128, 256), BF),
            jax.ShapeDtypeStruct((1, 128, 256), BF),
        ),
        in_specs=[pl.BlockSpec(memory_space=pl.ANY)] * 6 + [pl.BlockSpec(memory_space=pltpu.SMEM)],
        out_specs=(vmem, vmem, vmem),
        scratch_shapes=[
            pltpu.VMEM((8, 2, 512, 128), BF),
            pltpu.VMEM((2, 512, 128), BF),
            pltpu.VMEM((8, 2, 2, 128, 128), BF),
            pltpu.VMEM((8, 2, 2, 128, 128), BF),
            pltpu.VMEM((8, 2, 128, 128), BF),
            pltpu.VMEM((8, 2, 128, 128), BF),
            pltpu.VMEM((8, 2, 2, 128, 128), F32),
            pltpu.VMEM((8, 2, 128, 128), BF),
            pltpu.VMEM((4, 2, 2, 128, 128), BF),
            pltpu.VMEM((2, 4, 2, 128, 128), BF),
            pltpu.VMEM((2, 4, 2, 128, 128), BF),
            pltpu.VMEM((2, 128, 128), F32),
            pltpu.VMEM((2, 2, 4, 128), F32),
            pltpu.VMEM((3, 128, 1024), BF),
            pltpu.VMEM((3, 128, 1024), BF),
            pltpu.VMEM((128, 1024), BF),
            pltpu.VMEM((128, 1024), BF),
            pltpu.VMEM((8, 256, 128), BF),
            pltpu.VMEM((8, 256, 128), BF),
            pltpu.VMEM((8, 256, 256), BF),
            pltpu.VMEM((8, 256, 256), BF),
            pltpu.VMEM((8, 128, 256), F32),
            pltpu.VMEM((128, 512), BF),
            pltpu.VMEM((512, 128), F32),
            pltpu.VMEM((512, 128), F32),
            pltpu.VMEM((512, 128), BF),
            dma((2, 2)), dma((3,)), dma, dma, dma((3, 2)), dma((8,)), dma((8, 2)), dma((8, 2)), dma((8, 2)), dma((8, 2)),
            dma((8, 2)), dma((8, 2)), dma((8, 2)), dma((8, 2)), dma((8,)), dma((4, 2)), dma((2, 4)), dma((2, 4)),
            dma((4,)), dma((2, 2)), dma((3,)), dma((3,)), dma, dma,
        ],
        compiler_params=pltpu.CompilerParams(
            collective_id=0, has_side_effects=True, vmem_limit_bytes=56 * 2**20
        ),
    )(queries, keys, values, outputs, output_gradient, log_norms, doc_lengths)


def passed_along(x, axis, by):
    peers = lax.axis_size(axis)
    return lax.ppermute(x, axis, [(i, (i + by) % peers) for i in range(peers)])


def shifted(block, axis, distance):
    devices = range(lax.axis_size(axis))
    route = [(i - distance, i) for i in devices if i - distance in devices]
    return lax.ppermute(block, axis, route)


def doc_starts(doc_lengths, positions):
    firsts = jnp.cumsum(doc_lengths) - doc_lengths
    return jnp.max(jnp.where(firsts[None, :] <= positions[:, None], firsts[None, :], 0), axis=1)


def pass_grads(key_gradient_total, total_value_gradient):
    return passed_along((key_gradient_total, total_value_gradient), "blk", 1)


def scattered_sum(x):
    parts = x.reshape(4, x.shape[0] // 4, x.shape[1])
    return jnp.sum(lax.all_to_all(parts, "head", split_axis=0, concat_axis=0), axis=0)


def ring(queries, keys, values, outputs, output_gradient, log_norms, doc_lengths):
    block_count = lax.axis_size("blk")
    block_index = lax.axis_index("blk")
    every_query, every_output, grad_all = (
        lax.all_to_all(queries, "head", split_axis=2, concat_axis=1, tiled=True),
        lax.all_to_all(outputs, "head", split_axis=2, concat_axis=1, tiled=True),
        lax.all_to_all(output_gradient, "head", split_axis=2, concat_axis=1, tiled=True),
    )
    rows_per_block = every_query.shape[1]
    head_features = keys.shape[2] // KEY_VALUE_HEADS
    local_heads = every_query.shape[2] // head_features
    query_group_size = QUERY_HEADS // KEY_VALUE_HEADS
    logit_scale = head_features ** (-0.5)
    query_loc = every_query[0].reshape(rows_per_block, local_heads, head_features)
    grad_loc = grad_all[0].reshape(rows_per_block, local_heads, head_features)
    output_loc = every_output[0].reshape(rows_per_block, local_heads, head_features)
    row_delta = jnp.sum(grad_loc.astype(jnp.float32) * output_loc.astype(jnp.float32), axis=-1).T
    row_statistics = log_norms[0]
    kv_head = lax.axis_index("head") * local_heads // query_group_size
    key_own = lax.dynamic_slice_in_dim(keys[0], kv_head * head_features, head_features, 1)
    value_own = lax.dynamic_slice_in_dim(values[0], kv_head * head_features, head_features, 1)
    query_pos = block_index * rows_per_block + jnp.arange(rows_per_block, dtype=jnp.int32)
    first_pos = doc_starts(doc_lengths, query_pos)

    def tile_grads(pair, key_block):
        key_blk, value_blk = pair
        key_pos = key_block * rows_per_block + jnp.arange(rows_per_block, dtype=jnp.int32)
        allowed = (key_pos[None, :] <= query_pos[:, None]) & (
            key_pos[None, :] >= first_pos[:, None]
        )
        scores = logit_scale * jnp.einsum(
            "qhd,kd->hqk", query_loc, key_blk, preferred_element_type=jnp.float32
        )
        probability = jnp.where(allowed[None], jnp.exp(scores - row_statistics[:, :, None]), 0.0)
        prob_low = probability.astype(jnp.bfloat16)
        value_add = jnp.einsum(
            "hqk,qhd->kd", prob_low, grad_loc, preferred_element_type=jnp.float32
        )
        dprob = jnp.einsum("qhd,kd->hqk", grad_loc, value_blk, preferred_element_type=jnp.float32)
        dscore = (probability * (dprob - row_delta[:, :, None])).astype(jnp.bfloat16)
        query_add = jnp.einsum("hqk,kd->qhd", dscore, key_blk, preferred_element_type=jnp.float32)
        key_increment = jnp.einsum(
            "hqk,qhd->kd", dscore, query_loc, preferred_element_type=jnp.float32
        )
        return (query_add, key_increment, value_add)

    def no_grads():
        flat = jnp.zeros((rows_per_block, head_features), jnp.float32)
        return (jnp.zeros((rows_per_block, local_heads, head_features), jnp.float32), flat, flat)

    def visit_block(carry_state, cycle_step):
        pair, query_acc, key_gradient_total, total_value_gradient = carry_state
        key_block = (block_index - cycle_step) % block_count
        active = (key_block <= block_index) & ((key_block + 1) * rows_per_block - 1 >= first_pos[0])
        query_add, key_increment, value_add = lax.cond(
            active, lambda: tile_grads(pair, key_block), no_grads
        )
        return (
            pair,
            query_acc + query_add,
            key_gradient_total + key_increment,
            total_value_gradient + value_add,
        )

    def cycle_turn(cycle_step, carry_state):
        pair, query_acc, key_gradient_total, total_value_gradient = visit_block(
            carry_state, cycle_step
        )
        pair = shifted((pair[0], pair[1]), "blk", 1)
        key_gradient_total, total_value_gradient = pass_grads(
            key_gradient_total, total_value_gradient
        )
        return (pair, query_acc, key_gradient_total, total_value_gradient)

    flat_zero = jnp.zeros((rows_per_block, head_features), jnp.float32)
    initial = (
        (key_own, value_own),
        jnp.zeros((rows_per_block, local_heads, head_features), jnp.float32),
        flat_zero,
        flat_zero,
    )
    carry_state = lax.fori_loop(0, block_count - 1, cycle_turn, initial)
    pair, query_acc, key_gradient_total, total_value_gradient = visit_block(
        carry_state, block_count - 1
    )
    key_gradient_total, total_value_gradient = pass_grads(key_gradient_total, total_value_gradient)
    broad_zeros = jnp.zeros((rows_per_block, KEY_VALUE_HEADS * head_features), jnp.float32)
    key_broadcast = lax.dynamic_update_slice_in_dim(
        broad_zeros, key_gradient_total, kv_head * head_features, 1
    )
    value_wide = lax.dynamic_update_slice_in_dim(
        broad_zeros, total_value_gradient, kv_head * head_features, 1
    )
    key_part, value_part = scattered_sum(key_broadcast), scattered_sum(value_wide)
    keys_gradient = (logit_scale * key_part).astype(jnp.bfloat16)[None]
    values_gradient = value_part.astype(jnp.bfloat16)[None]
    query_out = (
        (logit_scale * query_acc)
        .astype(jnp.bfloat16)
        .reshape(1, rows_per_block, local_heads * head_features)
    )
    query_grad = lax.all_to_all(query_out, "head", split_axis=1, concat_axis=2, tiled=True)
    return (query_grad, keys_gradient, values_gradient)


def store_kernel(*refs):
    moves = [
        pltpu.make_async_copy(refs[i], refs[3 + i], refs[6].at[i]) for i in range(3)
    ]
    for move in moves:
        move.start()
    for move in moves:
        move.wait()


def store(*results):
    anywhere = pl.BlockSpec(memory_space=pl.ANY)
    return pl.pallas_call(
        store_kernel,
        out_shape=tuple(jax.ShapeDtypeStruct(x.shape, x.dtype) for x in results),
        in_specs=[anywhere] * 3,
        out_specs=(anywhere,) * 3,
        scratch_shapes=[pltpu.SemaphoreType.DMA((3,))],
    )(*results)


def shards(*arrays):
    lengths = arrays[-1]
    later = lax.broadcasted_iota(jnp.int32, lengths.shape, 0) > 0
    short = jnp.max(jnp.where(later, lengths, 0)) <= 1537
    return store(*lax.cond(short, fused, ring, *arrays))


def solution(mesh):
    in_specs = (
        P("blk", "head", None),
        P("blk", None, None),
        P("blk", None, None),
        P("blk", "head", None),
        P("blk", "head", None),
        P("blk", "head", None),
        P(),
    )
    out_specs = (P("blk", "head", None), P("blk", "head", None), P("blk", "head", None))
    return jax.shard_map(shards, mesh=mesh, in_specs=in_specs, out_specs=out_specs, check_vma=False)
```
